512 devices in a mesh: chan: 64 (over y, x, core), band: 8 (over z).
Axes of the slice: x: 4, y: 8, z: 8, core: 2. Of those that a mesh axis runs over, the one named last changes fastest.
Arguments:
- traces: bfloat16 [64, 128, 32768], P(None, 'band', 'chan'), may hold values from -6 to 6
- window_starts: int32 [64], replicated, may hold values from 0 to 32512
- tile_offsets: int32 [64, 4], P('chan'), may hold values from 0 to 3, as said below
- tile_count: int32 [64], P('chan'), may hold values from 1 to 4, as said below
Outputs:
- correlations: bfloat16 [64, 4, 128, 128, 201], P('chan', None, 'band')
The draws below stay inside these ranges and needn't reach their ends.
Inputs may be any that keep to these rules, and one draw needn't show every extreme that they name: `tile_offsets`: in row c the first tile_count[c] entries are distinct offsets d in increasing order with c + d < 64; the other entries are 0. `tile_count`: block 0 has all 4 slots live; the last block has one.
All inputs are finite; a program needn't handle non-finite values.
Results may differ from the reference program's by a relative error of at most 0.0077.
Values may be sent and summed in bfloat16 or wider, within the bound.
No kernel may reach another device: no remote copies, remote signals or barrier semaphores. Data moves between devices by JAX's collectives and lax.ppermute only.
A program may use at most 64 MiB of HBM per device.

```python
import math
import jax
import jax.numpy as jnp
from jax import lax

CB = 128
RANGE = 300
WIN = 256
LAGS = 201
NWIN = 64
BLOCKS = 64
CH = 8192
T_SIZE = 32768
DMAX = 3
TMAX = 4


def tile_table(key):
    blocks = CH // CB
    index = jnp.arange(blocks, dtype=jnp.int32)
    usable = jnp.minimum(DMAX, blocks - 1 - index) + 1
    wanted = jax.random.randint(jax.random.fold_in(key, 11), (blocks,), 1, TMAX + 1)
    counts = jnp.minimum(wanted, usable).at[0].set(TMAX)
    slots = jnp.arange(TMAX, dtype=jnp.int32)
    scores = jax.random.randint(jax.random.fold_in(key, 12), (blocks, TMAX), 0, 1 << 20) * TMAX + slots[None, :]
    scores = jnp.where(slots[None, :] < usable[:, None], scores, (1 << 20) * TMAX + slots[None, :])
    order = jnp.argsort(scores, axis=1).astype(jnp.int32)
    live = slots[None, :] < counts[:, None]
    chosen = jnp.sort(jnp.where(live, order, TMAX + 1), axis=1)
    offsets = jnp.where(live, chosen, 0)
    return (offsets.astype(jnp.int32), counts.astype(jnp.int32))


def draw_tile_offsets(key, part):
    offsets, counts = tile_table(key)
    return offsets


def draw_tile_count(key, part):
    offsets, counts = tile_table(key)
    return counts


def plant(result, rng, least, top_value):
    longest = result.shape.index(max(result.shape))
    spots = []
    for shift in (0, 1):
        where = [jax.random.randint(jax.random.fold_in(rng, axis), (), 0, length) for axis, length in enumerate(result.shape)]
        where[longest] = (where[longest] + shift) % result.shape[longest]
        spots.append(tuple(where))
    return result.at[spots[0]].set(least).at[spots[1]].set(top_value)


def block_scale(own_key, shape, cuts, least, high):
    def one(position, shards_of):
        heights = jax.random.uniform(jax.random.fold_in(jax.random.fold_in(own_key, 6), position), (shards_of,), jnp.float32, least / len(cuts), high / len(cuts))
        return jnp.repeat(jnp.exp(heights), shape[position] // shards_of).reshape((-1,) + (1,) * (len(shape) - position - 1))

    level = one(*cuts[0])
    for cut in cuts[1:]:
        level = level * one(*cut)
    return level


def noise(stream_key, extent, scale, reach, split=(), kind=jnp.bfloat16):
    factor_of = block_scale(stream_key, extent, split, -0.22, 0.18) if split else 1.0
    entries = jax.random.normal(stream_key, extent, jnp.float32) * scale * factor_of
    return jnp.minimum(jnp.maximum(entries, -reach), reach).astype(kind)


def setup_inputs(seed: int = 0) -> dict:
    key_of = jax.random.split(jax.random.key(seed), 5)
    return {
        "traces": noise(key_of[0], (BLOCKS, CB, T_SIZE), 1.0, 6.0, ((1, 8), (2, 64))),
        "window_starts": plant(jax.random.randint(key_of[1], (NWIN,), 0, T_SIZE - WIN + 1), jax.random.fold_in(key_of[1], 1), 0, T_SIZE - WIN).astype(jnp.int32),
        "tile_offsets": draw_tile_offsets(jax.random.fold_in(key_of[4], 71), 0),
        "tile_count": draw_tile_count(jax.random.fold_in(key_of[4], 71), 0),
    }


EPS = 1e-06

def tables():
    times = jnp.arange(WIN, dtype=jnp.int32)
    bins = jnp.arange(WIN // 2, dtype=jnp.int32)
    hann = 0.5 - 0.5 * jnp.cos(2.0 * math.pi * times.astype(jnp.float32) / WIN)
    phase = 2.0 * math.pi * (times[:, None] * bins[None, :] % WIN).astype(jnp.float32) / WIN
    forward = jnp.concatenate([hann[:, None] * jnp.cos(phase), -hann[:, None] * jnp.sin(phase)], axis=1).astype(jnp.bfloat16)
    shifts = jnp.arange(LAGS, dtype=jnp.int32) - (LAGS - 1) // 2
    turn = 2.0 * math.pi * (bins[:, None] * shifts[None, :] % WIN).astype(jnp.float32) / WIN
    factor = jnp.where(bins == 0, 1.0, 2.0).astype(jnp.float32)[:, None]
    inverse = jnp.concatenate([factor * jnp.cos(turn), -factor * jnp.sin(turn)], axis=0).astype(jnp.bfloat16)
    return (forward, inverse)

def reference(traces, window_starts, tile_offsets, tile_count):
    forward, inverse = tables()
    half = WIN // 2
    blocks = traces.shape[0]

    def whiten(series):
        windows = jax.vmap(lambda begin: lax.dynamic_slice_in_dim(series, begin, WIN, 1))(window_starts)
        spectra = jnp.einsum('wct,tk->kcw', windows.astype(jnp.float32), forward.astype(jnp.float32)).astype(jnp.bfloat16)
        parts = spectra.astype(jnp.float32).reshape(2, half, series.shape[0], window_starts.shape[0])
        power = lax.optimization_barrier(jnp.mean(parts[0] * parts[0] + parts[1] * parts[1], axis=2))
        return (parts * lax.rsqrt(power + EPS)[None, :, :, None]).astype(jnp.bfloat16)
    whites = lax.map(whiten, traces)
    table = inverse.astype(jnp.float32).reshape(2, half, LAGS)
    rows_idx = jnp.arange(CB, dtype=jnp.int32)

    def block_corr(block):
        mine = whites[block].astype(jnp.float32)

        def per_slot(slot):
            offset = tile_offsets[block, slot]
            other = whites[jnp.minimum(block + offset, blocks - 1)].astype(jnp.float32)
            real_part = jnp.einsum('fiw,fjw->fij', mine[0], other[0]) + jnp.einsum('fiw,fjw->fij', mine[1], other[1])
            imag_part = jnp.einsum('fiw,fjw->fij', mine[0], other[1]) - jnp.einsum('fiw,fjw->fij', mine[1], other[0])
            spread = offset * CB + rows_idx[None, :] - rows_idx[:, None]
            keep = ((spread > 0) & (spread <= RANGE) & (slot < tile_count[block])).astype(jnp.float32)
            cross = (jnp.stack([real_part, imag_part]) / NWIN * keep[None, None]).astype(jnp.bfloat16)
            return jnp.einsum('xkij,xkl->ijl', cross.astype(jnp.float32), table).astype(jnp.bfloat16)
        return lax.map(per_slot, jnp.arange(TMAX, dtype=jnp.int32))
    return lax.map(block_corr, jnp.arange(blocks, dtype=jnp.int32))
```

```python
import math

import jax
import jax.numpy as jnp
import numpy as np
from jax import lax
from jax.experimental import pallas as pl
from jax.experimental.pallas import tpu as pltpu
from jax.sharding import PartitionSpec as P

CB = 128
RANGE = 300
WIN = 256
HALF = WIN // 2
LAGS = 201
NWIN = 64
TMAX = 4
LANES = 128
LAG_ROWS = 208
EPS = 1e-06
MIB = 1 << 20


def tables(bands):
    f32 = np.float32
    turn = f32(2.0 * math.pi)
    times = np.arange(WIN)
    bins = np.arange(HALF)
    hann = f32(0.5) - f32(0.5) * np.cos(turn * times.astype(f32) / f32(WIN))
    phase = turn * (times[:, None] * bins[None, :] % WIN).astype(f32) / f32(WIN)
    forward = np.concatenate([hann[:, None] * np.cos(phase), -hann[:, None] * np.sin(phase)], axis=1)
    shifts = np.arange(LAGS) - (LAGS - 1) // 2
    angle = turn * (bins[:, None] * shifts[None, :] % WIN).astype(f32) / f32(WIN)
    factor = np.where(bins == 0, 1.0, 2.0).astype(f32)[:, None]
    inverse = np.stack([factor * np.cos(angle), -factor * np.sin(angle)], axis=0)
    width = HALF // bands
    inverse = inverse.reshape(2, bands, width, LAGS).transpose(1, 0, 2, 3).reshape(WIN, LAGS)
    inverse = np.pad(inverse.T, ((0, LAG_ROWS - LAGS), (0, 0)))
    return (
        jnp.asarray(forward.T.astype(jnp.bfloat16)),
        jnp.asarray(inverse.astype(jnp.bfloat16)),
    )


NT = (((1,), (1,)), ((), ()))
NN = (((1,), (0,)), ((), ()))


def dot(a, b, dims):
    return lax.dot_general(a, b, dims, preferred_element_type=jnp.float32)


def spectra_kernel(starts, traces, forward, out, seg0, seg1, white):
    rows, samples = traces.shape[1], traces.shape[2]
    chunks = samples // LANES
    last = traces.shape[0] * chunks - 1
    lane = lax.broadcasted_iota(jnp.int32, (rows, LANES), 1)

    def cut(w, carry):
        begin = starts[w]
        first = begin // LANES
        shift = begin % LANES

        def chunk(index):
            index = jnp.minimum(index, last)
            at = pl.multiple_of((index % chunks) * LANES, LANES)
            piece = traces[index // chunks, :, pl.ds(at, LANES)].astype(jnp.float32)
            return pltpu.roll(piece, (LANES - shift) % LANES, 1)

        a, b, c = chunk(first), chunk(first + 1), chunk(first + 2)
        inside = lane < LANES - shift
        seg0[pl.ds(w, rows, stride=NWIN), :] = jnp.where(inside, a, b)
        seg1[pl.ds(w, rows, stride=NWIN), :] = jnp.where(inside, b, c)
        return carry

    lax.fori_loop(0, NWIN, cut, 0, unroll=4)
    real_lane = lax.broadcasted_iota(jnp.int32, (HALF, 2 * LANES), 1) % LANES < NWIN

    def transform(pair, carry):
        at = pl.multiple_of(pair * LANES, LANES)
        both = jnp.concatenate([seg0[pl.ds(at, LANES), :], seg1[pl.ds(at, LANES), :]], axis=1)
        both = both.astype(jnp.bfloat16).reshape(2, NWIN, WIN)
        twice = jnp.concatenate([both, both], axis=1).reshape(4 * NWIN, WIN)
        result = dot(forward[...], twice, NT)
        spectra = jnp.where(real_lane, result[:HALF], result[HALF:])
        spectra = spectra.astype(jnp.bfloat16).astype(jnp.float32)
        for half in range(2):
            mine = spectra[:, half * LANES : (half + 1) * LANES]
            power = jnp.sum(mine * mine, axis=1, keepdims=True) * (1.0 / NWIN)
            white[pl.ds(2 * pair + half, HALF, stride=rows), :] = mine * lax.rsqrt(power + EPS)
        return carry

    lax.fori_loop(0, rows // 2, transform, 0)
    out[...] = white[...].astype(jnp.bfloat16).reshape(out.shape)


def whitened_rows(starts, series, forward, bands):
    rows = series.shape[1]
    width = HALF // bands
    return pl.pallas_call(
        spectra_kernel,
        out_shape=jax.ShapeDtypeStruct((bands, width, rows, LANES), jnp.bfloat16),
        in_specs=[
            pl.BlockSpec(memory_space=pltpu.SMEM),
            pl.BlockSpec(memory_space=pltpu.VMEM),
            pl.BlockSpec(memory_space=pltpu.VMEM),
        ],
        out_specs=pl.BlockSpec(memory_space=pltpu.VMEM),
        scratch_shapes=[
            pltpu.VMEM((rows * NWIN, LANES), jnp.float32),
            pltpu.VMEM((rows * NWIN, LANES), jnp.float32),
            pltpu.VMEM((HALF * rows, LANES), jnp.float32),
        ],
        compiler_params=pltpu.CompilerParams(vmem_limit_bytes=16 * MIB),
    )(starts, series, forward)


def both_sides(own, f):
    mine = own[:, f].reshape(CB, LANES)
    wide = mine.astype(jnp.float32)
    lane = lax.broadcasted_iota(jnp.int32, (CB, LANES), 1)
    turned = pltpu.roll(wide, NWIN, 1)
    turned = jnp.where(lane < NWIN, -turned, turned).astype(jnp.bfloat16)
    return mine, jnp.concatenate([mine, turned], axis=0)


def near_kernel(own, next1, out, held):
    bands, width, rows = own.shape[:3]

    def one(f, carry):
        mine, sides = both_sides(own, f)
        result = dot(sides, next1[:, f].reshape(CB, LANES), NT) * (1.0 / NWIN)
        held[pl.ds(f, CB, stride=2 * width), :] = result[:CB]
        held[pl.ds(width + f, CB, stride=2 * width), :] = result[CB:]
        return carry

    lax.fori_loop(0, width, one, 0)
    out[...] = held[...].astype(jnp.bfloat16).reshape(out.shape)


def far_kernel(own, next2, next3, out, held0, held1):
    bands, width, rows = own.shape[:3]
    half = rows // 2
    tail = next3.shape[0]
    step = 2 * width
    row_index = lax.broadcasted_iota(jnp.int32, (CB, LANES), 0)
    column = lax.broadcasted_iota(jnp.int32, (CB, LANES), 1)
    after = column > row_index
    left = lax.broadcasted_iota(jnp.int32, (bands, half, LANES), 2) < LANES // 2
    blank = jnp.zeros((CB // 2 - tail * rows, LANES), jnp.bfloat16)

    def one(f, carry):
        mine, sides = both_sides(own, f)
        second = next2[:, f].reshape(CB, LANES)
        low = second[: CB // 2]
        third = next3[:, f].reshape(tail * rows, LANES)
        mixed = jnp.concatenate([mine, second[CB // 2 :], third, blank, low, low], axis=0)
        result = dot(sides, mixed, NT) * (1.0 / NWIN)
        for part in range(2):
            of = result[part * CB : (part + 1) * CB]
            shared = jnp.where(after, of[:, :CB], of[:, CB : 2 * CB])
            split = of[:, 2 * CB :].reshape(bands, 2, half, LANES)
            folded = jnp.where(left, split[:, 0], split[:, 1]).reshape(bands * half, LANES)
            held0[pl.ds(part * width + f, CB, stride=step), :] = shared
            held1[pl.ds(part * width + f, CB // 2, stride=step), :] = folded
        return carry

    lax.fori_loop(0, width, one, 0)
    out[:, :rows] = held0[...].astype(jnp.bfloat16).reshape(bands, rows, step, LANES)
    out[:, rows:] = held1[...].astype(jnp.bfloat16).reshape(bands, half, step, LANES)


def vmem_call(kernel, out_shape, scratch, limit, *args):
    return pl.pallas_call(
        kernel,
        out_shape=jax.ShapeDtypeStruct(out_shape, jnp.bfloat16),
        in_specs=[pl.BlockSpec(memory_space=pltpu.VMEM)] * len(args),
        out_specs=pl.BlockSpec(memory_space=pltpu.VMEM),
        scratch_shapes=[pltpu.VMEM(shape, jnp.float32) for shape in scratch],
        compiler_params=pltpu.CompilerParams(vmem_limit_bytes=limit),
    )(*args)


def lag_kernel(info, near, far, inverse, out, held):
    bands, rows, step = near.shape[:3]
    half = rows // 2
    depth = bands * step
    first = info[2 * TMAX]
    column = lax.broadcasted_iota(jnp.int32, (LAG_ROWS, LANES), 1)
    table = inverse[...]

    def put(offset, row, value):
        held[info[offset], pl.ds(row, LAGS, stride=rows), :] = value[:LAGS]

    def one(low_row, carry):
        high_row = low_row + half
        pieces = [
            near[:, low_row],
            near[:, high_row],
            far[:, low_row],
            far[:, high_row],
            far[:, rows + low_row],
        ]
        pieces = [piece.reshape(depth, LANES) for piece in pieces]
        near_pair = dot(table, jnp.concatenate(pieces[:2], axis=1), NN)
        shared_pair = dot(table, jnp.concatenate(pieces[2:4], axis=1), NN)
        folded = dot(table, pieces[4], NN)
        for k, row in enumerate((low_row, high_row)):
            put(1, row, near_pair[:, k * LANES : (k + 1) * LANES])
            shared = shared_pair[:, k * LANES : (k + 1) * LANES]
            i = first + row
            put(0, row, jnp.where(column > i, shared, 0.0))
            turned = pltpu.roll(shared, LANES // 2, 1)
            lower = folded if k == 0 else pltpu.roll(folded, LANES // 2, 1)
            joined = jnp.where(column < LANES // 2, lower, turned)
            put(2, row, jnp.where(column <= i + RANGE - 2 * CB, joined, 0.0))
            put(3, row, jnp.where(column <= i + RANGE - 3 * CB, turned, 0.0))
        return carry

    lax.fori_loop(0, half, one, 0)
    for slot in range(TMAX):
        live = info[TMAX + slot] > 0

        @pl.when(live)
        def _():
            out[slot] = held[slot].astype(jnp.bfloat16).reshape(LAGS, rows, LANES)

        @pl.when(jnp.logical_not(live))
        def _():
            out[slot] = jnp.zeros((LAGS, rows, LANES), jnp.bfloat16)


def lags(info, near, far, inverse):
    rows = near.shape[1]
    return pl.pallas_call(
        lag_kernel,
        out_shape=jax.ShapeDtypeStruct((TMAX, LAGS, rows, LANES), jnp.bfloat16),
        in_specs=[pl.BlockSpec(memory_space=pltpu.SMEM)]
        + [pl.BlockSpec(memory_space=pltpu.VMEM)] * 3,
        out_specs=pl.BlockSpec(memory_space=pltpu.VMEM),
        scratch_shapes=[pltpu.VMEM((TMAX + 1, LAGS * rows, LANES), jnp.float32)],
        compiler_params=pltpu.CompilerParams(vmem_limit_bytes=32 * MIB),
    )(info, near, far, inverse)


def passed_along(block, axis, distance):
    devices = range(lax.axis_size(axis))
    route = [(i - distance, i) for i in devices if i - distance in devices]
    return lax.ppermute(block, axis, route)


def exchanged(block, axis):
    return lax.all_to_all(block, axis, split_axis=0, concat_axis=0, tiled=True)


def local(traces, window_starts, tile_offsets, tile_count):
    bands = lax.axis_size("band")
    rows = CB // bands
    width = HALF // bands
    forward, inverse = tables(bands)
    series = exchanged(traces, "chan")
    own = exchanged(whitened_rows(window_starts, series, forward, bands), "band")
    next1 = passed_along(own, "chan", -1)
    next2 = passed_along(own, "chan", -2)
    reach = -(-(RANGE - 2 * CB) // rows)
    next3 = passed_along(own[:reach], "chan", -3)
    tile = (bands, rows, 2 * width, LANES)
    near = vmem_call(near_kernel, tile, [(CB * 2 * width, LANES)], 16 * MIB, own, next1)
    near = exchanged(near, "band")
    far = vmem_call(
        far_kernel,
        (bands, rows + rows // 2, 2 * width, LANES),
        [(CB * 2 * width, LANES), (CB // 2 * 2 * width, LANES)],
        24 * MIB,
        own,
        next2,
        next3,
    )
    far = exchanged(far, "band")
    live = jnp.arange(TMAX) < tile_count[0]
    holds = (tile_offsets[0][None, :] == jnp.arange(TMAX)[:, None]) & live[None, :]
    slot_of = jnp.where(holds.any(axis=1), jnp.argmax(holds, axis=1), TMAX)
    first = (lax.axis_index("band") * rows)[None]
    info = jnp.concatenate([slot_of, live, first]).astype(jnp.int32)
    result = lags(info, near, far, inverse)
    return result.transpose(0, 2, 3, 1)[None]


def solution(mesh):
    placed = (P(None, "band", "chan"), P(), P("chan", None), P("chan"))
    return jax.shard_map(
        local,
        mesh=mesh,
        in_specs=placed,
        out_specs=P("chan", None, "band", None, None),
        check_vma=False,
    )
```

```python
import math

import jax
import jax.numpy as jnp
import numpy as np
from jax import lax
from jax.experimental import pallas as pl
from jax.experimental.pallas import tpu as pltpu
from jax.sharding import PartitionSpec as P

CB = 128
RANGE = 300
WIN = 256
HALF = WIN // 2
LAGS = 201
NWIN = 64
TMAX = 4
LANES = 128
LAG_ROWS = 208
EPS = 1e-06
MIB = 1 << 20


def tables(bands):
    f32 = np.float32
    turn = f32(2.0 * math.pi)
    times = np.arange(WIN)
    bins = np.arange(HALF)
    hann = f32(0.5) - f32(0.5) * np.cos(turn * times.astype(f32) / f32(WIN))
    phase = turn * (times[:, None] * bins[None, :] % WIN).astype(f32) / f32(WIN)
    forward = np.concatenate([hann[:, None] * np.cos(phase), -hann[:, None] * np.sin(phase)], axis=1)
    shifts = np.arange(LAGS) - (LAGS - 1) // 2
    angle = turn * (bins[:, None] * shifts[None, :] % WIN).astype(f32) / f32(WIN)
    factor = np.where(bins == 0, 1.0, 2.0).astype(f32)[:, None]
    inverse = np.stack([factor * np.cos(angle), -factor * np.sin(angle)], axis=0)
    width = HALF // bands
    inverse = inverse.reshape(2, bands, width, LAGS).transpose(1, 0, 2, 3).reshape(WIN, LAGS)
    inverse = np.pad(inverse.T, ((0, LAG_ROWS - LAGS), (0, 0)))
    return (
        jnp.asarray(forward.T.astype(jnp.bfloat16)),
        jnp.asarray(inverse.astype(jnp.bfloat16)),
    )


NT = (((1,), (1,)), ((), ()))
NN = (((1,), (0,)), ((), ()))


def dot(a, b, dims):
    return lax.dot_general(a, b, dims, preferred_element_type=jnp.float32)


def spectra_kernel(starts, traces, forward, out, seg0, seg1, white):
    rows, samples = traces.shape[1], traces.shape[2]
    chunks = samples // LANES
    last = traces.shape[0] * chunks - 1
    lane = lax.broadcasted_iota(jnp.int32, (rows, LANES), 1)

    def cut(w, carry):
        begin = starts[w]
        first = begin // LANES
        shift = begin % LANES

        def chunk(index):
            index = jnp.minimum(index, last)
            at = pl.multiple_of((index % chunks) * LANES, LANES)
            piece = traces[index // chunks, :, pl.ds(at, LANES)].astype(jnp.float32)
            return pltpu.roll(piece, (LANES - shift) % LANES, 1)

        a, b, c = chunk(first), chunk(first + 1), chunk(first + 2)
        inside = lane < LANES - shift
        seg0[pl.ds(w, rows, stride=NWIN), :] = jnp.where(inside, a, b)
        seg1[pl.ds(w, rows, stride=NWIN), :] = jnp.where(inside, b, c)
        return carry

    lax.fori_loop(0, NWIN, cut, 0, unroll=True)
    real_lane = lax.broadcasted_iota(jnp.int32, (HALF, 2 * LANES), 1) % LANES < NWIN

    def transform(pair, carry):
        at = pl.multiple_of(pair * LANES, LANES)
        both = jnp.concatenate([seg0[pl.ds(at, LANES), :], seg1[pl.ds(at, LANES), :]], axis=1)
        both = both.astype(jnp.bfloat16).reshape(2, NWIN, WIN)
        twice = jnp.concatenate([both, both], axis=1).reshape(4 * NWIN, WIN)
        result = dot(forward[...], twice, NT)
        spectra = jnp.where(real_lane, result[:HALF], result[HALF:])
        spectra = spectra.astype(jnp.bfloat16).astype(jnp.float32)
        for half in range(2):
            mine = spectra[:, half * LANES : (half + 1) * LANES]
            power = jnp.sum(mine * mine, axis=1, keepdims=True) * (1.0 / NWIN)
            white[pl.ds(2 * pair + half, HALF, stride=rows), :] = mine * lax.rsqrt(power + EPS)
        return carry

    lax.fori_loop(0, rows // 2, transform, 0, unroll=True)
    out[...] = white[...].astype(jnp.bfloat16).reshape(out.shape)


def whitened_rows(starts, series, forward, bands):
    rows = series.shape[1]
    width = HALF // bands
    return pl.pallas_call(
        spectra_kernel,
        out_shape=jax.ShapeDtypeStruct((bands, width, rows, LANES), jnp.bfloat16),
        in_specs=[
            pl.BlockSpec(memory_space=pltpu.SMEM),
            pl.BlockSpec(memory_space=pltpu.VMEM),
            pl.BlockSpec(memory_space=pltpu.VMEM),
        ],
        out_specs=pl.BlockSpec(memory_space=pltpu.VMEM),
        scratch_shapes=[
            pltpu.VMEM((rows * NWIN, LANES), jnp.float32),
            pltpu.VMEM((rows * NWIN, LANES), jnp.float32),
            pltpu.VMEM((HALF * rows, LANES), jnp.float32),
        ],
        compiler_params=pltpu.CompilerParams(vmem_limit_bytes=16 * MIB),
    )(starts, series, forward)


def both_sides(own, f):
    mine = own[:, f].reshape(CB, LANES)
    wide = mine.astype(jnp.float32)
    lane = lax.broadcasted_iota(jnp.int32, (CB, LANES), 1)
    turned = pltpu.roll(wide, NWIN, 1)
    turned = jnp.where(lane < NWIN, -turned, turned).astype(jnp.bfloat16)
    return mine, jnp.concatenate([mine, turned], axis=0)


def near_kernel(own, next1, out, held):
    bands, width, rows = own.shape[:3]

    def one(f, carry):
        mine, sides = both_sides(own, f)
        result = dot(sides, next1[:, f].reshape(CB, LANES), NT) * (1.0 / NWIN)
        held[pl.ds(f, CB, stride=2 * width), :] = result[:CB]
        held[pl.ds(width + f, CB, stride=2 * width), :] = result[CB:]
        return carry

    lax.fori_loop(0, width, one, 0, unroll=True)
    out[...] = held[...].astype(jnp.bfloat16).reshape(out.shape)


def far_kernel(own, next2_even, next2_odd, next3, out, held0, held1):
    bands, width, rows = own.shape[:3]
    half = rows // 2
    tail = next3.shape[0]
    step = 2 * width
    row_index = lax.broadcasted_iota(jnp.int32, (CB, LANES), 0)
    column = lax.broadcasted_iota(jnp.int32, (CB, LANES), 1)
    after = column > row_index
    left = lax.broadcasted_iota(jnp.int32, (bands, half, LANES), 2) < LANES // 2
    blank = jnp.zeros((CB // 2 - tail * rows, LANES), jnp.bfloat16)

    def one(f, carry):
        mine, sides = both_sides(own, f)
        second = (next2_even[:, f] + next2_odd[:, f]).reshape(CB, LANES)
        low = second[: CB // 2]
        third = next3[:, f].reshape(tail * rows, LANES)
        mixed = jnp.concatenate([mine, second[CB // 2 :], third, blank, low, low], axis=0)
        result = dot(sides, mixed, NT) * (1.0 / NWIN)
        for part in range(2):
            of = result[part * CB : (part + 1) * CB]
            shared = jnp.where(after, of[:, :CB], of[:, CB : 2 * CB])
            split = of[:, 2 * CB :].reshape(bands, 2, half, LANES)
            folded = jnp.where(left, split[:, 0], split[:, 1]).reshape(bands * half, LANES)
            held0[pl.ds(part * width + f, CB, stride=step), :] = shared
            held1[pl.ds(part * width + f, CB // 2, stride=step), :] = folded
        return carry

    lax.fori_loop(0, width, one, 0, unroll=True)
    out[:, :rows] = held0[...].astype(jnp.bfloat16).reshape(bands, rows, step, LANES)
    out[:, rows:] = held1[...].astype(jnp.bfloat16).reshape(bands, half, step, LANES)


def vmem_call(kernel, out_shape, scratch, limit, *args):
    return pl.pallas_call(
        kernel,
        out_shape=jax.ShapeDtypeStruct(out_shape, jnp.bfloat16),
        in_specs=[pl.BlockSpec(memory_space=pltpu.VMEM)] * len(args),
        out_specs=pl.BlockSpec(memory_space=pltpu.VMEM),
        scratch_shapes=[pltpu.VMEM(shape, jnp.float32) for shape in scratch],
        compiler_params=pltpu.CompilerParams(vmem_limit_bytes=limit),
    )(*args)


def near_lag_kernel(near, inverse, out, held):
    bands, rows, step = near.shape[:3]
    table = inverse[...]

    def one(pair, carry):
        pieces = [near[:, 2 * pair + k].reshape(bands * step, LANES) for k in range(2)]
        result = dot(table, jnp.concatenate(pieces, axis=1), NN)
        for k in range(2):
            value = result[:LAGS, k * LANES : (k + 1) * LANES]
            held[pl.ds(2 * pair + k, LAGS, stride=rows), :] = value
        return carry

    lax.fori_loop(0, rows // 2, one, 0, unroll=True)
    out[...] = held[...].astype(jnp.bfloat16).reshape(out.shape)


def lag_kernel(info, near, far, inverse, out, held, done, sems):
    bands, rows, step = far.shape[0], near.shape[1], far.shape[2]
    half = rows // 2
    depth = bands * step
    first = info[2 * TMAX]
    column = lax.broadcasted_iota(jnp.int32, (LAG_ROWS, LANES), 1)
    table = inverse[...]

    def send(offset, source):
        slot = info[offset]

        @pl.when(slot < TMAX)
        def _():
            pltpu.make_async_copy(source, out.at[slot], sems.at[slot]).start()

    send(1, near)
    done[0] = jnp.zeros(done.shape[1:], jnp.bfloat16)
    for slot in range(TMAX):

        @pl.when(info[TMAX + slot] == 0)
        def _():
            pltpu.make_async_copy(done.at[0], out.at[slot], sems.at[slot]).start()

    def put(place, row, value):
        held[place, pl.ds(row, LAGS, stride=rows), :] = value[:LAGS]

    def one(low_row, carry):
        high_row = low_row + half
        pieces = [far[:, low_row], far[:, high_row], far[:, rows + low_row]]
        pieces = [piece.reshape(depth, LANES) for piece in pieces]
        shared_pair = dot(table, jnp.concatenate(pieces[:2], axis=1), NN)
        folded = dot(table, pieces[2], NN)
        for k, row in enumerate((low_row, high_row)):
            shared = shared_pair[:, k * LANES : (k + 1) * LANES]
            i = first + row
            put(0, row, jnp.where(column > i, shared, 0.0))
            turned = pltpu.roll(shared, LANES // 2, 1)
            lower = folded if k == 0 else pltpu.roll(folded, LANES // 2, 1)
            joined = jnp.where(column < LANES // 2, lower, turned)
            put(1, row, jnp.where(column <= i + RANGE - 2 * CB, joined, 0.0))
            put(2, row, jnp.where(column <= i + RANGE - 3 * CB, turned, 0.0))
        return carry

    lax.fori_loop(0, half, one, 0, unroll=True)
    for place, offset in enumerate((0, 2, 3)):
        done[1 + place] = held[place].astype(jnp.bfloat16).reshape(LAGS, rows, LANES)
        send(offset, done.at[1 + place])
    for slot in range(TMAX):
        pltpu.make_async_copy(done.at[0], out.at[slot], sems.at[slot]).wait()


def lags(info, near, far, inverse):
    rows = near.shape[1]
    return pl.pallas_call(
        lag_kernel,
        out_shape=jax.ShapeDtypeStruct((TMAX, LAGS, rows, LANES), jnp.bfloat16),
        in_specs=[pl.BlockSpec(memory_space=pltpu.SMEM)]
        + [pl.BlockSpec(memory_space=pltpu.VMEM)] * 3,
        out_specs=pl.BlockSpec(memory_space=pl.ANY),
        scratch_shapes=[
            pltpu.VMEM((TMAX - 1, LAGS * rows, LANES), jnp.float32),
            pltpu.VMEM((TMAX, LAGS, rows, LANES), jnp.bfloat16),
            pltpu.SemaphoreType.DMA((TMAX,)),
        ],
        compiler_params=pltpu.CompilerParams(vmem_limit_bytes=32 * MIB),
    )(info, near, far, inverse)


def from_ahead(block, distance, parity=None):
    count = lax.axis_size("chan")
    route = [(i + distance, i) for i in range(count - distance) if parity is None or i % 2 == parity]
    return lax.ppermute(block, "chan", route)


def exchanged(block, axis):
    return lax.all_to_all(block, axis, split_axis=0, concat_axis=0, tiled=True)


def local(traces, window_starts, tile_offsets, tile_count):
    bands = lax.axis_size("band")
    rows = CB // bands
    width = HALF // bands
    forward, inverse = tables(bands)
    series = exchanged(traces, "chan")
    own = exchanged(whitened_rows(window_starts, series, forward, bands), "band")
    next1 = from_ahead(own, 1)
    next2 = (from_ahead(next1, 1, 0), from_ahead(own, 2, 1))
    reach = -(-(RANGE - 2 * CB) // rows)
    next3 = from_ahead(own[:reach], 3)
    tile = (bands, rows, 2 * width, LANES)
    near = vmem_call(near_kernel, tile, [(CB * 2 * width, LANES)], 16 * MIB, own, next1)
    near = exchanged(near, "band")
    near = vmem_call(
        near_lag_kernel, (LAGS, rows, LANES), [(LAGS * rows, LANES)], 16 * MIB, near, inverse
    )
    far = vmem_call(
        far_kernel,
        (bands, rows + rows // 2, 2 * width, LANES),
        [(CB * 2 * width, LANES), (CB // 2 * 2 * width, LANES)],
        24 * MIB,
        own,
        *next2,
        next3,
    )
    far = exchanged(far, "band")
    live = jnp.arange(TMAX) < tile_count[0]
    holds = (tile_offsets[0][None, :] == jnp.arange(TMAX)[:, None]) & live[None, :]
    slot_of = jnp.where(holds.any(axis=1), jnp.argmax(holds, axis=1), TMAX)
    first = (lax.axis_index("band") * rows)[None]
    info = jnp.concatenate([slot_of, live, first]).astype(jnp.int32)
    result = lags(info, near, far, inverse)
    return result.transpose(0, 2, 3, 1)[None]


def solution(mesh):
    placed = (P(None, "band", "chan"), P(), P("chan", None), P("chan"))
    return jax.shard_map(
        local,
        mesh=mesh,
        in_specs=placed,
        out_specs=P("chan", None, "band", None, None),
        check_vma=False,
    )
```

```python
import math

import jax
import jax.numpy as jnp
import numpy as np
from jax import lax
from jax.experimental import pallas as pl
from jax.experimental.pallas import tpu as pltpu
from jax.sharding import PartitionSpec as P

CB = 128
RANGE = 300
WIN = 256
HALF = WIN // 2
LAGS = 201
NWIN = 64
TMAX = 4
LANES = 128
LAG_ROWS = 208
PACK = 304
LOW = PACK - 2 * CB
UNITS = 6
EPS = 1e-06
MIB = 1 << 20


def tables(bands):
    f32 = np.float32
    turn = f32(2.0 * math.pi)
    times = np.arange(WIN)
    bins = np.arange(HALF)
    hann = f32(0.5) - f32(0.5) * np.cos(turn * times.astype(f32) / f32(WIN))
    phase = turn * (times[:, None] * bins[None, :] % WIN).astype(f32) / f32(WIN)
    forward = np.concatenate([hann[:, None] * np.cos(phase), -hann[:, None] * np.sin(phase)], axis=1)
    shifts = np.arange(LAGS) - (LAGS - 1) // 2
    angle = turn * (bins[:, None] * shifts[None, :] % WIN).astype(f32) / f32(WIN)
    factor = np.where(bins == 0, 1.0, 2.0).astype(f32)[:, None]
    inverse = np.stack([factor * np.cos(angle), -factor * np.sin(angle)], axis=0)
    width = HALF // bands
    inverse = inverse.reshape(2, bands, width, LAGS).transpose(1, 0, 2, 3).reshape(WIN, LAGS)
    inverse = np.pad(inverse.T, ((0, LAG_ROWS - LAGS), (0, 0)))
    return (
        jnp.asarray(forward.T.astype(jnp.bfloat16)),
        jnp.asarray(inverse.astype(jnp.bfloat16)),
    )


NT = (((1,), (1,)), ((), ()))
NN = (((1,), (0,)), ((), ()))


def dot(a, b, dims):
    return lax.dot_general(a, b, dims, preferred_element_type=jnp.float32)


def spectra_kernel(starts, traces, forward, out, seg0, seg1, white):
    rows, samples = traces.shape[1], traces.shape[2]
    log_lanes = LANES.bit_length() - 1
    chunks = samples // LANES
    log_chunks = chunks.bit_length() - 1
    last = traces.shape[0] * chunks - 1
    lane = lax.broadcasted_iota(jnp.int32, (rows, LANES), 1)

    def cut(w, carry):
        begin = starts[w]
        first = lax.shift_right_logical(begin, log_lanes)
        shift = lax.bitwise_and(begin, LANES - 1)
        turn = lax.bitwise_and(LANES - shift, LANES - 1)

        def chunk(index):
            at = pl.multiple_of(lax.bitwise_and(index, chunks - 1) * LANES, LANES)
            shard = lax.shift_right_logical(index, log_chunks)
            piece = traces[shard, :, pl.ds(at, LANES)].astype(jnp.float32)
            return pltpu.roll(piece, turn, 1)

        a, b, c = chunk(first), chunk(first + 1), chunk(jnp.minimum(first + 2, last))
        inside = lane < LANES - shift
        seg0[pl.ds(w, rows, stride=NWIN), :] = jnp.where(inside, a, b)
        seg1[pl.ds(w, rows, stride=NWIN), :] = jnp.where(inside, b, c)
        return carry

    lax.fori_loop(0, NWIN, cut, 0, unroll=True)
    real_lane = lax.broadcasted_iota(jnp.int32, (HALF, 2 * LANES), 1) % LANES < NWIN

    def transform(pair, carry):
        at = pl.multiple_of(pair * LANES, LANES)
        both = jnp.concatenate([seg0[pl.ds(at, LANES), :], seg1[pl.ds(at, LANES), :]], axis=1)
        both = both.astype(jnp.bfloat16).reshape(2, NWIN, WIN)
        twice = jnp.concatenate([both, both], axis=1).reshape(4 * NWIN, WIN)
        result = dot(forward[...], twice, NT)
        spectra = jnp.where(real_lane, result[:HALF], result[HALF:])
        spectra = spectra.astype(jnp.bfloat16).astype(jnp.float32)
        for half in range(2):
            mine = spectra[:, half * LANES : (half + 1) * LANES]
            power = jnp.sum(mine * mine, axis=1, keepdims=True) * (1.0 / NWIN)
            white[pl.ds(2 * pair + half, HALF, stride=rows), :] = mine * lax.rsqrt(power + EPS)
        return carry

    lax.fori_loop(0, rows // 2, transform, 0, unroll=True)
    out[...] = white[...].astype(jnp.bfloat16).reshape(out.shape)


def whitened_rows(starts, series, forward, bands):
    rows = series.shape[1]
    width = HALF // bands
    return pl.pallas_call(
        spectra_kernel,
        out_shape=jax.ShapeDtypeStruct((bands, width, rows, LANES), jnp.bfloat16),
        in_specs=[
            pl.BlockSpec(memory_space=pltpu.SMEM),
            pl.BlockSpec(memory_space=pltpu.VMEM),
            pl.BlockSpec(memory_space=pltpu.VMEM),
        ],
        out_specs=pl.BlockSpec(memory_space=pltpu.VMEM),
        scratch_shapes=[
            pltpu.VMEM((rows * NWIN, LANES), jnp.float32),
            pltpu.VMEM((rows * NWIN, LANES), jnp.float32),
            pltpu.VMEM((HALF * rows, LANES), jnp.float32),
        ],
        compiler_params=pltpu.CompilerParams(vmem_limit_bytes=16 * MIB),
    )(starts, series, forward)


def both_sides(own, f):
    mine = own[:, f].reshape(CB, LANES)
    wide = mine.astype(jnp.float32)
    lane = lax.broadcasted_iota(jnp.int32, (CB, LANES), 1)
    turned = pltpu.roll(wide, NWIN, 1)
    turned = jnp.where(lane < NWIN, -turned, turned).astype(jnp.bfloat16)
    return mine, jnp.concatenate([mine, turned], axis=0)


def near_kernel(own, next1, out):
    bands, width, rows = own.shape[:3]

    def one(f, carry):
        mine, sides = both_sides(own, f)
        result = dot(sides, next1[:, f].reshape(CB, LANES), NT) * (1.0 / NWIN)
        result = result.astype(jnp.bfloat16).reshape(2, bands, rows, LANES)
        out[:, f] = result[0]
        out[:, width + f] = result[1]
        return carry

    lax.fori_loop(0, width, one, 0, unroll=True)


def far_kernel(own, next2_even, next2_odd, next3, out, held0, held1, plain, tail):
    bands, width, rows = own.shape[:3]
    step = 2 * width
    row_index = lax.broadcasted_iota(jnp.int32, (CB, LANES), 0)
    column = lax.broadcasted_iota(jnp.int32, (CB, LANES), 1)
    after = column > row_index
    lane = lax.broadcasted_iota(jnp.int32, (bands, LANES), 1)

    def one(f, carry):
        mine, sides = both_sides(own, f)
        second = (next2_even[:, f] + next2_odd[:, f]).reshape(CB, LANES)
        low = second[:LOW]
        third = next3[:, f].reshape(LOW, LANES)
        mixed = [mine, second[LOW:], third, low, low, low[:32], low, low, low[32:], low[32:]]
        result = dot(sides, jnp.concatenate(mixed, axis=0), NT) * (1.0 / NWIN)
        for part in range(2):
            of = result[part * CB : (part + 1) * CB]
            at = part * width + f
            held0[pl.ds(at, CB, stride=step), :] = jnp.where(after, of[:, :CB], of[:, CB : 2 * CB])
            base = pl.multiple_of(at * CB, CB)
            plain[pl.ds(base, CB), :] = of[:, 2 * CB : 3 * CB]
            tail[pl.ds(base, CB), :] = of[:, 3 * CB :]

            def row(ref, r):
                return ref[pl.ds(base + r, bands, stride=rows), :]

            for unit in range(UNITS):
                if unit < 4:
                    last = row(plain, 12 + unit)
                else:
                    pair = 12 + 2 * (unit - 4)
                    last = jnp.where(lane < LANES - 16, row(tail, pair), row(tail, pair + 1))
                value = jnp.where(lane < 2 * LOW, row(plain, UNITS + unit), last)
                value = jnp.where(lane < LOW, row(plain, unit), value)
                held1[pl.ds(unit * step + at, bands, stride=UNITS * step), :] = value
        return carry

    lax.fori_loop(0, width, one, 0, unroll=True)
    out[:, :rows] = held0[...].astype(jnp.bfloat16).reshape(bands, rows, step, LANES)
    out[:, rows:] = held1[...].astype(jnp.bfloat16).reshape(bands, UNITS, step, LANES)


def vmem_call(kernel, out_shape, scratch, limit, *args):
    return pl.pallas_call(
        kernel,
        out_shape=jax.ShapeDtypeStruct(out_shape, jnp.bfloat16),
        in_specs=[pl.BlockSpec(memory_space=pltpu.VMEM)] * len(args),
        out_specs=pl.BlockSpec(memory_space=pltpu.VMEM),
        scratch_shapes=[pltpu.VMEM(shape, jnp.float32) for shape in scratch],
        compiler_params=pltpu.CompilerParams(vmem_limit_bytes=limit),
    )(*args)


def near_lag_kernel(near, inverse, out, wide, held):
    bands, step, rows = near.shape[:3]
    depth = bands * step
    table = inverse[...]
    wide[...] = near[...].astype(jnp.float32).reshape(wide.shape)

    def one(pair, carry):
        pieces = [
            wide[pl.ds(2 * pair + k, depth, stride=rows), :].astype(jnp.bfloat16) for k in range(2)
        ]
        result = dot(table, jnp.concatenate(pieces, axis=1), NN)
        for k in range(2):
            value = result[:LAGS, k * LANES : (k + 1) * LANES]
            held[pl.ds(2 * pair + k, LAGS, stride=rows), :] = value
        return carry

    lax.fori_loop(0, rows // 2, one, 0, unroll=True)
    out[...] = held[...].astype(jnp.bfloat16).reshape(out.shape)


def lag_kernel(info, near, far, inverse, out, held, low, done, sems):
    bands, rows, step = far.shape[0], near.shape[1], far.shape[2]
    depth = bands * step
    first = info[2 * TMAX]
    column = lax.broadcasted_iota(jnp.int32, (LAG_ROWS, LANES), 1)
    table = inverse[...]

    def send(offset, source):
        slot = info[offset]

        @pl.when(slot < TMAX)
        def _():
            pltpu.make_async_copy(source, out.at[slot], sems.at[slot]).start()

    send(1, near)
    done[0] = jnp.zeros(done.shape[1:], jnp.bfloat16)
    for slot in range(TMAX):

        @pl.when(info[TMAX + slot] == 0)
        def _():
            pltpu.make_async_copy(done.at[0], out.at[slot], sems.at[slot]).start()

    def piece(row):
        return far[:, row].reshape(depth, LANES)

    def paired(row):
        both = dot(table, jnp.concatenate([piece(row), piece(row + 1)], axis=1), NN)
        return both[:, :LANES], both[:, LANES:]

    for unit in range(0, UNITS, 2):
        low[unit], low[unit + 1] = paired(rows + unit)

    def lower(row):
        if row < UNITS:
            return low[row]
        if row < 2 * UNITS:
            return pltpu.roll(low[row - UNITS], LANES - LOW, 1)
        extra = row - 2 * UNITS
        start = pltpu.roll(low[extra], 32, 1)
        end = pltpu.roll(low[4 + extra // 2], 64 - 16 * (extra % 2), 1)
        return jnp.where(column < 32, start, end)

    def put(place, row, value):
        held[place, pl.ds(row, LAGS, stride=rows), :] = value[:LAGS]

    for pair in range(0, rows, 2):
        for row, shared in zip((pair, pair + 1), paired(pair)):
            i = first + row
            put(0, row, jnp.where(column > i, shared, 0.0))
            turned = pltpu.roll(shared, LOW, 1)
            joined = jnp.where(column < LOW, lower(row), turned)
            put(1, row, jnp.where(column <= i + RANGE - 2 * CB, joined, 0.0))
            put(2, row, jnp.where(column <= i + RANGE - 3 * CB, turned, 0.0))

    for place, offset in enumerate((0, 2, 3)):
        done[1 + place] = held[place].astype(jnp.bfloat16).reshape(LAGS, rows, LANES)
        send(offset, done.at[1 + place])
    for slot in range(TMAX):
        pltpu.make_async_copy(done.at[0], out.at[slot], sems.at[slot]).wait()


def lags(info, near, far, inverse):
    rows = near.shape[1]
    return pl.pallas_call(
        lag_kernel,
        out_shape=jax.ShapeDtypeStruct((TMAX, LAGS, rows, LANES), jnp.bfloat16),
        in_specs=[pl.BlockSpec(memory_space=pltpu.SMEM)]
        + [pl.BlockSpec(memory_space=pltpu.VMEM)] * 3,
        out_specs=pl.BlockSpec(memory_space=pl.ANY),
        scratch_shapes=[
            pltpu.VMEM((TMAX - 1, LAGS * rows, LANES), jnp.float32),
            pltpu.VMEM((UNITS, LAG_ROWS, LANES), jnp.float32),
            pltpu.VMEM((TMAX, LAGS, rows, LANES), jnp.bfloat16),
            pltpu.SemaphoreType.DMA((TMAX,)),
        ],
        compiler_params=pltpu.CompilerParams(vmem_limit_bytes=32 * MIB),
    )(info, near, far, inverse)


def from_ahead(block, distance, parity=None):
    count = lax.axis_size("chan")
    route = [(i + distance, i) for i in range(count - distance) if parity is None or i % 2 == parity]
    return lax.ppermute(block, "chan", route)


def exchanged(block, axis):
    return lax.all_to_all(block, axis, split_axis=0, concat_axis=0, tiled=True)


def local(traces, window_starts, tile_offsets, tile_count):
    bands = lax.axis_size("band")
    rows = CB // bands
    width = HALF // bands
    forward, inverse = tables(bands)
    series = exchanged(traces, "chan")
    own = exchanged(whitened_rows(window_starts, series, forward, bands), "band")
    next1 = from_ahead(own, 1)
    next2 = (from_ahead(next1, 1, 0), from_ahead(own, 2, 1))
    reach = -(-(RANGE - 2 * CB) // rows)
    next3 = from_ahead(own[:reach], 3)
    near = vmem_call(near_kernel, (bands, 2 * width, rows, LANES), [], 16 * MIB, own, next1)
    near = exchanged(near, "band")
    near = vmem_call(
        near_lag_kernel,
        (LAGS, rows, LANES),
        [(WIN * rows, LANES), (LAGS * rows, LANES)],
        16 * MIB,
        near,
        inverse,
    )
    far = vmem_call(
        far_kernel,
        (bands, rows + UNITS, 2 * width, LANES),
        [
            (CB * 2 * width, LANES),
            (bands * UNITS * 2 * width, LANES),
            (CB * 2 * width, LANES),
            (CB * 2 * width, LANES),
        ],
        24 * MIB,
        own,
        *next2,
        next3,
    )
    far = exchanged(far, "band")
    live = jnp.arange(TMAX) < tile_count[0]
    holds = (tile_offsets[0][None, :] == jnp.arange(TMAX)[:, None]) & live[None, :]
    slot_of = jnp.where(holds.any(axis=1), jnp.argmax(holds, axis=1), TMAX)
    first = (lax.axis_index("band") * rows)[None]
    info = jnp.concatenate([slot_of, live, first]).astype(jnp.int32)
    result = lags(info, near, far, inverse)
    return result.transpose(0, 2, 3, 1)[None]


def solution(mesh):
    placed = (P(None, "band", "chan"), P(), P("chan", None), P("chan"))
    return jax.shard_map(
        local,
        mesh=mesh,
        in_specs=placed,
        out_specs=P("chan", None, "band", None, None),
        check_vma=False,
    )
```

```python
import math

import jax
import jax.numpy as jnp
import numpy as np
from jax import lax
from jax.experimental import pallas as pl
from jax.experimental.pallas import tpu as pltpu
from jax.sharding import PartitionSpec as P

CB = 128
RANGE = 300
WIN = 256
HALF = WIN // 2
LAGS = 201
NWIN = 64
TMAX = 4
LANES = 128
LAG_ROWS = 208
PACK = 304
LOW = PACK - 2 * CB
GROUP = 16
UNITS = 4
EPS = 1e-06
MIB = 1 << 20


def tables(bands):
    f32 = np.float32
    turn = f32(2.0 * math.pi)
    times = np.arange(WIN)
    bins = np.arange(HALF)
    hann = f32(0.5) - f32(0.5) * np.cos(turn * times.astype(f32) / f32(WIN))
    phase = turn * (times[:, None] * bins[None, :] % WIN).astype(f32) / f32(WIN)
    forward = np.concatenate([hann[:, None] * np.cos(phase), -hann[:, None] * np.sin(phase)], axis=1)
    shifts = np.arange(LAGS) - (LAGS - 1) // 2
    angle = turn * (bins[:, None] * shifts[None, :] % WIN).astype(f32) / f32(WIN)
    factor = np.where(bins == 0, 1.0, 2.0).astype(f32)[:, None]
    inverse = np.stack([factor * np.cos(angle), -factor * np.sin(angle)], axis=0)
    width = HALF // bands
    inverse = inverse.reshape(2, bands, width, LAGS).transpose(1, 0, 2, 3).reshape(WIN, LAGS)
    inverse = np.pad(inverse.T, ((0, LAG_ROWS - LAGS), (0, 0)))
    return (
        jnp.asarray(forward.T.astype(jnp.bfloat16)),
        jnp.asarray(inverse.astype(jnp.bfloat16)),
    )


NT = (((1,), (1,)), ((), ()))
NN = (((1,), (0,)), ((), ()))


def dot(a, b, dims):
    return lax.dot_general(a, b, dims, preferred_element_type=jnp.float32)


def spectra_kernel(starts, traces, forward, out, seg0, seg1, white):
    rows, samples = traces.shape[1], traces.shape[2]
    log_lanes = LANES.bit_length() - 1
    chunks = samples // LANES
    log_chunks = chunks.bit_length() - 1
    last = traces.shape[0] * chunks - 1
    lane = lax.broadcasted_iota(jnp.int32, (rows, LANES), 1)

    def cut(w, carry):
        begin = starts[w]
        first = lax.shift_right_logical(begin, log_lanes)
        shift = lax.bitwise_and(begin, LANES - 1)
        turn = lax.bitwise_and(LANES - shift, LANES - 1)

        def chunk(index):
            at = pl.multiple_of(lax.bitwise_and(index, chunks - 1) * LANES, LANES)
            shard = lax.shift_right_logical(index, log_chunks)
            piece = traces[shard, :, pl.ds(at, LANES)].astype(jnp.float32)
            return pltpu.roll(piece, turn, 1)

        a, b, c = chunk(first), chunk(first + 1), chunk(jnp.minimum(first + 2, last))
        inside = lane < LANES - shift
        seg0[pl.ds(w, rows, stride=NWIN), :] = jnp.where(inside, a, b)
        seg1[pl.ds(w, rows, stride=NWIN), :] = jnp.where(inside, b, c)
        return carry

    lax.fori_loop(0, NWIN, cut, 0, unroll=True)
    real_lane = lax.broadcasted_iota(jnp.int32, (HALF, 2 * LANES), 1) % LANES < NWIN

    def transform(pair, carry):
        at = pl.multiple_of(pair * LANES, LANES)
        both = jnp.concatenate([seg0[pl.ds(at, LANES), :], seg1[pl.ds(at, LANES), :]], axis=1)
        both = both.astype(jnp.bfloat16).reshape(2, NWIN, WIN)
        twice = jnp.concatenate([both, both], axis=1).reshape(4 * NWIN, WIN)
        result = dot(forward[...], twice, NT)
        spectra = jnp.where(real_lane, result[:HALF], result[HALF:])
        spectra = spectra.astype(jnp.bfloat16).astype(jnp.float32)
        for half in range(2):
            mine = spectra[:, half * LANES : (half + 1) * LANES]
            power = jnp.sum(mine * mine, axis=1, keepdims=True) * (1.0 / NWIN)
            white[pl.ds(2 * pair + half, HALF, stride=rows), :] = mine * lax.rsqrt(power + EPS)
        return carry

    lax.fori_loop(0, rows // 2, transform, 0, unroll=True)
    out[...] = white[...].astype(jnp.bfloat16).reshape(out.shape)


def whitened_rows(starts, series, forward, bands):
    rows = series.shape[1]
    width = HALF // bands
    return pl.pallas_call(
        spectra_kernel,
        out_shape=jax.ShapeDtypeStruct((bands, width, rows, LANES), jnp.bfloat16),
        in_specs=[
            pl.BlockSpec(memory_space=pltpu.SMEM),
            pl.BlockSpec(memory_space=pltpu.VMEM),
            pl.BlockSpec(memory_space=pltpu.VMEM),
        ],
        out_specs=pl.BlockSpec(memory_space=pltpu.VMEM),
        scratch_shapes=[
            pltpu.VMEM((rows * NWIN, LANES), jnp.float32),
            pltpu.VMEM((rows * NWIN, LANES), jnp.float32),
            pltpu.VMEM((HALF * rows, LANES), jnp.float32),
        ],
        compiler_params=pltpu.CompilerParams(vmem_limit_bytes=16 * MIB),
    )(starts, series, forward)


def both_sides(own, f):
    mine = own[:, f].reshape(CB, LANES)
    wide = mine.astype(jnp.float32)
    lane = lax.broadcasted_iota(jnp.int32, (CB, LANES), 1)
    turned = pltpu.roll(wide, NWIN, 1)
    turned = jnp.where(lane < NWIN, -turned, turned).astype(jnp.bfloat16)
    return mine, jnp.concatenate([mine, turned], axis=0)


def near_kernel(own, next1, out):
    bands, width, rows = own.shape[:3]

    def one(f, carry):
        mine, sides = both_sides(own, f)
        result = dot(sides, next1[:, f].reshape(CB, LANES), NT) * (1.0 / NWIN)
        result = result.astype(jnp.bfloat16).reshape(2, bands, rows, LANES)
        out[:, f] = result[0]
        out[:, width + f] = result[1]
        return carry

    lax.fori_loop(0, width, one, 0, unroll=True)


def far_kernel(own, next2_even, next2_odd, next3, out, held0, held1, plain):
    bands, width, rows = own.shape[:3]
    step = 2 * width
    row_index = lax.broadcasted_iota(jnp.int32, (CB, LANES), 0)
    column = lax.broadcasted_iota(jnp.int32, (CB, LANES), 1)
    after = column > row_index
    band = row_index // GROUP
    hole = column // GROUP == band - LOW // GROUP
    second_half = column // GROUP % 2 == 1
    lane = lax.broadcasted_iota(jnp.int32, (bands, LANES), 1)

    def one(f, carry):
        mine, sides = both_sides(own, f)
        second = (next2_even[:, f] + next2_odd[:, f]).reshape(CB, LANES)
        third = next3[:, f].reshape(LOW, LANES)
        copies = LANES // GROUP
        low = [second[k * GROUP : (k + 1) * GROUP] for k in range(3) for _ in range(copies)]
        mixed = jnp.concatenate([mine, second[LOW:], third] + low, axis=0)
        result = dot(sides, mixed, NT) * (1.0 / NWIN)
        for part in range(2):
            of = result[part * CB : (part + 1) * CB]
            at = part * width + f
            here, there, low0, low1, low2 = (of[:, k * CB : (k + 1) * CB] for k in range(5))
            shared = jnp.where(hole, low2, jnp.where(after, here, there))
            held0[pl.ds(at, CB, stride=step), :] = shared
            left = jnp.where(band == 0, low1, low0)
            right = jnp.where(band <= 1, low2, low1)
            base = at * CB
            plain[pl.ds(base, CB), :] = jnp.where(second_half, right, left)
            for unit in range(UNITS):
                value = plain[pl.ds(base + unit + 12, bands, stride=rows), :]
                for k in (2, 1, 0):
                    other = plain[pl.ds(base + unit + 4 * k, bands, stride=rows), :]
                    value = jnp.where(lane < 32 * (k + 1), other, value)
                held1[pl.ds(unit * step + at, bands, stride=UNITS * step), :] = value
        return carry

    lax.fori_loop(0, width, one, 0, unroll=True)
    out[:, :rows] = held0[...].astype(jnp.bfloat16).reshape(bands, rows, step, LANES)
    out[:, rows:] = held1[...].astype(jnp.bfloat16).reshape(bands, UNITS, step, LANES)


def local_kernel(first, mine, other, inverse, out, held):
    bands, width, rows = mine.shape[:3]
    copies = LANES // GROUP
    lane = lax.broadcasted_iota(jnp.int32, (rows, LANES), 1)
    row_index = lax.broadcasted_iota(jnp.int32, (rows, LANES), 0)
    wanted = lane // GROUP == row_index % copies

    def one(f, carry):
        for band in range(bands):
            rows_of = mine[band, f]
            wide = rows_of.astype(jnp.float32)
            turned = pltpu.roll(wide, NWIN, 1)
            turned = jnp.where(lane < NWIN, -turned, turned).astype(jnp.bfloat16)
            sides = jnp.concatenate([rows_of, turned], axis=0)
            columns = jnp.concatenate([other[band, f]] * copies, axis=0)
            result = dot(sides, columns, NT) * (1.0 / NWIN)
            for part in range(2):
                picked = jnp.where(wanted, result[part * rows : (part + 1) * rows], 0.0)
                for half in range(2):
                    line = jnp.sum(picked[half * copies : (half + 1) * copies], axis=0, keepdims=True)
                    held[half, pl.ds(band * 2 * width + part * width + f, 1), :] = line
        return carry

    lax.fori_loop(0, width, one, 0)
    for half in range(2):
        result = dot(inverse[...], held[half].astype(jnp.bfloat16), NN)
        for k in range(copies):
            turn = lax.bitwise_and(first[0] + (LANES - GROUP * k), LANES - 1)
            out[half * copies + k] = pltpu.roll(result, turn, 1)


def local_lags(first, mine, other, inverse):
    return pl.pallas_call(
        local_kernel,
        out_shape=jax.ShapeDtypeStruct((mine.shape[2], LAG_ROWS, LANES), jnp.float32),
        in_specs=[pl.BlockSpec(memory_space=pltpu.SMEM)]
        + [pl.BlockSpec(memory_space=pltpu.VMEM)] * 3,
        out_specs=pl.BlockSpec(memory_space=pltpu.VMEM),
        scratch_shapes=[pltpu.VMEM((2, WIN, LANES), jnp.float32)],
        compiler_params=pltpu.CompilerParams(vmem_limit_bytes=16 * MIB),
    )(first, mine, other, inverse)


def vmem_call(kernel, out_shape, scratch, limit, *args):
    return pl.pallas_call(
        kernel,
        out_shape=jax.ShapeDtypeStruct(out_shape, jnp.bfloat16),
        in_specs=[pl.BlockSpec(memory_space=pltpu.VMEM)] * len(args),
        out_specs=pl.BlockSpec(memory_space=pltpu.VMEM),
        scratch_shapes=[pltpu.VMEM(shape, jnp.float32) for shape in scratch],
        compiler_params=pltpu.CompilerParams(vmem_limit_bytes=limit),
    )(*args)


def near_lag_kernel(near, inverse, out, wide, held):
    bands, step, rows = near.shape[:3]
    depth = bands * step
    table = inverse[...]
    wide[...] = near[...].astype(jnp.float32).reshape(wide.shape)

    def one(pair, carry):
        pieces = [
            wide[pl.ds(2 * pair + k, depth, stride=rows), :].astype(jnp.bfloat16) for k in range(2)
        ]
        result = dot(table, jnp.concatenate(pieces, axis=1), NN)
        for k in range(2):
            value = result[:LAGS, k * LANES : (k + 1) * LANES]
            held[pl.ds(2 * pair + k, LAGS, stride=rows), :] = value
        return carry

    lax.fori_loop(0, rows // 2, one, 0, unroll=True)
    out[...] = held[...].astype(jnp.bfloat16).reshape(out.shape)


def lag_kernel(info, near, same, far, inverse, out, held, parts, done, sems):
    bands, rows, step = far.shape[0], near.shape[1], far.shape[2]
    depth = bands * step
    first = info[2 * TMAX]
    column = lax.broadcasted_iota(jnp.int32, (LAG_ROWS, LANES), 1)
    table = inverse[...]

    def send(offset, source):
        slot = info[offset]

        @pl.when(slot < TMAX)
        def _():
            pltpu.make_async_copy(source, out.at[slot], sems.at[slot]).start()

    send(1, near)
    done[0] = jnp.zeros(done.shape[1:], jnp.bfloat16)
    for slot in range(TMAX):

        @pl.when(info[TMAX + slot] == 0)
        def _():
            pltpu.make_async_copy(done.at[0], out.at[slot], sems.at[slot]).start()

    def piece(row):
        return far[:, row].reshape(depth, LANES)

    def paired(row):
        both = dot(table, jnp.concatenate([piece(row), piece(row + 1)], axis=1), NN)
        return both[:, :LANES], both[:, LANES:]

    for unit in range(0, UNITS, 2):
        parts[unit], parts[unit + 1] = paired(rows + unit)
    own_group = (column >= first) & (column < first + GROUP)
    extra = (column >= jnp.where(first == 0, GROUP, 32)) & (column < LOW)
    has_hole = first >= LOW

    def lower(row):
        unit, at = row % UNITS, 32 * (row // UNITS)
        value = parts[unit]
        if at:
            value = pltpu.roll(value, LANES - at, 1)
        turn = jnp.where(has_hole, 32 + LOW + LANES - first, LANES - at + GROUP)
        moved = parts[jnp.where(has_hole, UNITS + row, unit)]
        return jnp.where(extra, pltpu.roll(moved, lax.bitwise_and(turn, LANES - 1), 1), value)

    def put(place, row, value):
        held[place, pl.ds(row, LAGS, stride=rows), :] = value[:LAGS]

    for pair in range(0, rows, 2):
        for row, shared in zip((pair, pair + 1), paired(pair)):
            i = first + row
            put(0, row, jnp.where(column > i, shared, 0.0))
            turned = pltpu.roll(shared, LOW, 1)
            parts[UNITS + row] = shared
            joined = jnp.where(column < LOW, lower(row), turned)
            joined = jnp.where(own_group, same[row], joined)
            put(1, row, jnp.where(column <= i + RANGE - 2 * CB, joined, 0.0))
            put(2, row, jnp.where(column <= i + RANGE - 3 * CB, turned, 0.0))

    for place, offset in enumerate((0, 2, 3)):
        done[1 + place] = held[place].astype(jnp.bfloat16).reshape(LAGS, rows, LANES)
        send(offset, done.at[1 + place])
    for slot in range(TMAX):
        pltpu.make_async_copy(done.at[0], out.at[slot], sems.at[slot]).wait()


def lags(info, near, same, far, inverse):
    rows = near.shape[1]
    return pl.pallas_call(
        lag_kernel,
        out_shape=jax.ShapeDtypeStruct((TMAX, LAGS, rows, LANES), jnp.bfloat16),
        in_specs=[
            pl.BlockSpec(memory_space=pltpu.SMEM),
            pl.BlockSpec(memory_space=pl.ANY),
            pl.BlockSpec(memory_space=pltpu.VMEM),
            pl.BlockSpec(memory_space=pltpu.VMEM),
            pl.BlockSpec(memory_space=pltpu.VMEM),
        ],
        out_specs=pl.BlockSpec(memory_space=pl.ANY),
        scratch_shapes=[
            pltpu.VMEM((TMAX - 1, LAGS * rows, LANES), jnp.float32),
            pltpu.VMEM((UNITS + rows, LAG_ROWS, LANES), jnp.float32),
            pltpu.VMEM((TMAX, LAGS, rows, LANES), jnp.bfloat16),
            pltpu.SemaphoreType.DMA((TMAX,)),
        ],
        compiler_params=pltpu.CompilerParams(vmem_limit_bytes=32 * MIB),
    )(info, near, same, far, inverse)


def from_ahead(block, distance, parity=None):
    count = lax.axis_size("chan")
    route = [(i + distance, i) for i in range(count - distance) if parity is None or i % 2 == parity]
    return lax.ppermute(block, "chan", route)


def exchanged(block, axis):
    return lax.all_to_all(block, axis, split_axis=0, concat_axis=0, tiled=True)


def local(traces, window_starts, tile_offsets, tile_count):
    bands = lax.axis_size("band")
    rows = CB // bands
    width = HALF // bands
    forward, inverse = tables(bands)
    series = exchanged(traces, "chan")
    white = whitened_rows(window_starts, series, forward, bands)
    own = exchanged(white, "band")
    next1 = from_ahead(own, 1)
    next2 = (from_ahead(next1, 1, 0), from_ahead(own, 2, 1))
    reach = -(-(RANGE - 2 * CB) // rows)
    next3 = from_ahead(own[:reach], 3)
    near = vmem_call(near_kernel, (bands, 2 * width, rows, LANES), [], 16 * MIB, own, next1)
    near = exchanged(near, "band")
    near = vmem_call(
        near_lag_kernel,
        (LAGS, rows, LANES),
        [(WIN * rows, LANES), (LAGS * rows, LANES)],
        16 * MIB,
        near,
        inverse,
    )
    far = vmem_call(
        far_kernel,
        (bands, rows + UNITS, 2 * width, LANES),
        [
            (CB * 2 * width, LANES),
            (bands * UNITS * 2 * width, LANES),
            (CB * 2 * width, LANES),
        ],
        24 * MIB,
        own,
        *next2,
        next3,
    )
    white, far = lax.optimization_barrier((white, far))
    first = (lax.axis_index("band") * rows).astype(jnp.int32)[None]
    same = local_lags(first, white, from_ahead(white, 2), inverse)
    far = exchanged(far, "band")
    live = jnp.arange(TMAX) < tile_count[0]
    holds = (tile_offsets[0][None, :] == jnp.arange(TMAX)[:, None]) & live[None, :]
    slot_of = jnp.where(holds.any(axis=1), jnp.argmax(holds, axis=1), TMAX)
    info = jnp.concatenate([slot_of, live, first]).astype(jnp.int32)
    near = pltpu.with_memory_space_constraint(near, pltpu.HBM)
    result = lags(info, near, same, far, inverse)
    return result.transpose(0, 2, 3, 1)[None]


def solution(mesh):
    placed = (P(None, "band", "chan"), P(), P("chan", None), P("chan"))
    return jax.shard_map(
        local,
        mesh=mesh,
        in_specs=placed,
        out_specs=P("chan", None, "band", None, None),
        check_vma=False,
    )
```

```python
import math

import jax
import jax.numpy as jnp
import numpy as np
from jax import lax
from jax.experimental import pallas as pl
from jax.experimental.pallas import tpu as pltpu
from jax.sharding import PartitionSpec as P

CB = 128
RANGE = 300
WIN = 256
HALF = WIN // 2
LAGS = 201
NWIN = 64
TMAX = 4
LANES = 128
LAG_ROWS = 208
PACK = 304
LOW = PACK - 2 * CB
GROUP = 16
UNITS = 4
EPS = 1e-06
MIB = 1 << 20


def tables(bands):
    f32 = np.float32
    turn = f32(2.0 * math.pi)
    times = np.arange(WIN)
    bins = np.arange(HALF)
    hann = f32(0.5) - f32(0.5) * np.cos(turn * times.astype(f32) / f32(WIN))
    phase = turn * (times[:, None] * bins[None, :] % WIN).astype(f32) / f32(WIN)
    forward = np.concatenate([hann[:, None] * np.cos(phase), -hann[:, None] * np.sin(phase)], axis=1)
    shifts = np.arange(LAGS) - (LAGS - 1) // 2
    angle = turn * (bins[:, None] * shifts[None, :] % WIN).astype(f32) / f32(WIN)
    factor = np.where(bins == 0, 1.0, 2.0).astype(f32)[:, None]
    inverse = np.stack([factor * np.cos(angle), -factor * np.sin(angle)], axis=0)
    width = HALF // bands
    inverse = inverse.reshape(2, bands, width, LAGS).transpose(1, 0, 2, 3).reshape(WIN, LAGS)
    inverse = np.pad(inverse.T, ((0, LAG_ROWS - LAGS), (0, 0)))
    return (
        jnp.asarray(forward.T.astype(jnp.bfloat16)),
        jnp.asarray(inverse.astype(jnp.bfloat16)),
    )


NT = (((1,), (1,)), ((), ()))
NN = (((1,), (0,)), ((), ()))


def dot(a, b, dims):
    return lax.dot_general(a, b, dims, preferred_element_type=jnp.float32)


def spectra_kernel(starts, traces, forward, out, seg0, seg1, white):
    rows, samples = traces.shape[1], traces.shape[2]
    log_lanes = LANES.bit_length() - 1
    chunks = samples // LANES
    log_chunks = chunks.bit_length() - 1
    last = traces.shape[0] * chunks - 1
    lane = lax.broadcasted_iota(jnp.int32, (rows, LANES), 1)

    def cut(w, carry):
        begin = starts[w]
        first = lax.shift_right_logical(begin, log_lanes)
        shift = lax.bitwise_and(begin, LANES - 1)
        turn = lax.bitwise_and(LANES - shift, LANES - 1)

        def chunk(index):
            at = pl.multiple_of(lax.bitwise_and(index, chunks - 1) * LANES, LANES)
            shard = lax.shift_right_logical(index, log_chunks)
            piece = traces[shard, :, pl.ds(at, LANES)].astype(jnp.float32)
            return pltpu.roll(piece, turn, 1)

        a, b, c = chunk(first), chunk(first + 1), chunk(jnp.minimum(first + 2, last))
        inside = lane < LANES - shift
        seg0[pl.ds(w, rows, stride=NWIN), :] = jnp.where(inside, a, b)
        seg1[pl.ds(w, rows, stride=NWIN), :] = jnp.where(inside, b, c)
        return carry

    lax.fori_loop(0, NWIN, cut, 0, unroll=True)
    real_lane = lax.broadcasted_iota(jnp.int32, (HALF, 2 * LANES), 1) % LANES < NWIN

    def transform(pair, carry):
        at = pl.multiple_of(pair * LANES, LANES)
        both = jnp.concatenate([seg0[pl.ds(at, LANES), :], seg1[pl.ds(at, LANES), :]], axis=1)
        both = both.astype(jnp.bfloat16).reshape(2, NWIN, WIN)
        twice = jnp.concatenate([both, both], axis=1).reshape(4 * NWIN, WIN)
        result = dot(forward[...], twice, NT)
        spectra = jnp.where(real_lane, result[:HALF], result[HALF:])
        spectra = spectra.astype(jnp.bfloat16).astype(jnp.float32)
        for half in range(2):
            mine = spectra[:, half * LANES : (half + 1) * LANES]
            power = jnp.sum(mine * mine, axis=1, keepdims=True) * (1.0 / NWIN)
            white[pl.ds(2 * pair + half, HALF, stride=rows), :] = mine * lax.rsqrt(power + EPS)
        return carry

    lax.fori_loop(0, rows // 2, transform, 0, unroll=True)
    out[...] = white[...].astype(jnp.bfloat16).reshape(out.shape)


def whitened_rows(starts, series, forward, bands):
    rows = series.shape[1]
    width = HALF // bands
    return pl.pallas_call(
        spectra_kernel,
        out_shape=jax.ShapeDtypeStruct((bands, width, rows, LANES), jnp.bfloat16),
        in_specs=[
            pl.BlockSpec(memory_space=pltpu.SMEM),
            pl.BlockSpec(memory_space=pltpu.VMEM),
            pl.BlockSpec(memory_space=pltpu.VMEM),
        ],
        out_specs=pl.BlockSpec(memory_space=pltpu.VMEM),
        scratch_shapes=[
            pltpu.VMEM((rows * NWIN, LANES), jnp.float32),
            pltpu.VMEM((rows * NWIN, LANES), jnp.float32),
            pltpu.VMEM((HALF * rows, LANES), jnp.float32),
        ],
        compiler_params=pltpu.CompilerParams(vmem_limit_bytes=16 * MIB),
    )(starts, series, forward)


def both_sides(own, f):
    mine = own[:, f].reshape(CB, LANES)
    wide = mine.astype(jnp.float32)
    lane = lax.broadcasted_iota(jnp.int32, (CB, LANES), 1)
    turned = pltpu.roll(wide, NWIN, 1)
    turned = jnp.where(lane < NWIN, -turned, turned).astype(jnp.bfloat16)
    return mine, jnp.concatenate([mine, turned], axis=0)


def near_kernel(own, next1, out):
    bands, width, rows = own.shape[:3]

    def one(f, carry):
        mine, sides = both_sides(own, f)
        result = dot(sides, next1[:, f].reshape(CB, LANES), NT) * (1.0 / NWIN)
        result = result.astype(jnp.bfloat16).reshape(2, bands, rows, LANES)
        out[:, f] = result[0]
        out[:, width + f] = result[1]
        return carry

    lax.fori_loop(0, width, one, 0, unroll=True)


def far_kernel(own, next2_even, next2_odd, next3, out, held0, held1, plain):
    bands, width, rows = own.shape[:3]
    step = 2 * width
    row_index = lax.broadcasted_iota(jnp.int32, (CB, LANES), 0)
    column = lax.broadcasted_iota(jnp.int32, (CB, LANES), 1)
    after = column > row_index
    band = row_index // GROUP
    hole = column // GROUP == band - LOW // GROUP
    second_half = column // GROUP % 2 == 1
    lane = lax.broadcasted_iota(jnp.int32, (bands, LANES), 1)

    def one(f, carry):
        mine, sides = both_sides(own, f)
        second = (next2_even[:, f] + next2_odd[:, f]).reshape(CB, LANES)
        third = next3[:, f].reshape(LOW, LANES)
        copies = LANES // GROUP
        low = [second[k * GROUP : (k + 1) * GROUP] for k in range(3) for _ in range(copies)]
        mixed = jnp.concatenate([mine, second[LOW:], third] + low, axis=0)
        result = dot(sides, mixed, NT) * (1.0 / NWIN)
        for part in range(2):
            of = result[part * CB : (part + 1) * CB]
            at = part * width + f
            here, there, low0, low1, low2 = (of[:, k * CB : (k + 1) * CB] for k in range(5))
            shared = jnp.where(hole, low2, jnp.where(after, here, there))
            held0[pl.ds(at, CB, stride=step), :] = shared
            left = jnp.where(band == 0, low1, low0)
            right = jnp.where(band <= 1, low2, low1)
            base = at * CB
            plain[pl.ds(base, CB), :] = jnp.where(second_half, right, left)
            for unit in range(UNITS):
                value = plain[pl.ds(base + unit + 12, bands, stride=rows), :]
                for k in (2, 1, 0):
                    other = plain[pl.ds(base + unit + 4 * k, bands, stride=rows), :]
                    value = jnp.where(lane < 32 * (k + 1), other, value)
                held1[pl.ds(unit * step + at, bands, stride=UNITS * step), :] = value
        return carry

    lax.fori_loop(0, width, one, 0, unroll=True)
    out[:, :rows] = held0[...].astype(jnp.bfloat16).reshape(bands, rows, step, LANES)
    out[:, rows:] = held1[...].astype(jnp.bfloat16).reshape(bands, UNITS, step, LANES)


def local_kernel(first, mine, other, inverse, out, held):
    bands, width, rows = mine.shape[:3]
    copies = LANES // GROUP
    lane = lax.broadcasted_iota(jnp.int32, (rows, LANES), 1)
    row_index = lax.broadcasted_iota(jnp.int32, (rows, LANES), 0)
    wanted = lane // GROUP == row_index % copies

    def one(f, carry):
        for band in range(bands):
            rows_of = mine[band, f]
            wide = rows_of.astype(jnp.float32)
            turned = pltpu.roll(wide, NWIN, 1)
            turned = jnp.where(lane < NWIN, -turned, turned).astype(jnp.bfloat16)
            sides = jnp.concatenate([rows_of, turned], axis=0)
            columns = jnp.concatenate([other[band, f]] * copies, axis=0)
            result = dot(sides, columns, NT) * (1.0 / NWIN)
            for part in range(2):
                picked = jnp.where(wanted, result[part * rows : (part + 1) * rows], 0.0)
                for half in range(2):
                    line = jnp.sum(picked[half * copies : (half + 1) * copies], axis=0, keepdims=True)
                    held[half, pl.ds(band * 2 * width + part * width + f, 1), :] = line
        return carry

    lax.fori_loop(0, width, one, 0)
    for half in range(2):
        result = dot(inverse[...], held[half].astype(jnp.bfloat16), NN)
        for k in range(copies):
            turn = lax.bitwise_and(first[0] + (LANES - GROUP * k), LANES - 1)
            out[half * copies + k] = pltpu.roll(result, turn, 1)


def local_lags(first, mine, other, inverse):
    return pl.pallas_call(
        local_kernel,
        out_shape=jax.ShapeDtypeStruct((mine.shape[2], LAG_ROWS, LANES), jnp.float32),
        in_specs=[pl.BlockSpec(memory_space=pltpu.SMEM)]
        + [pl.BlockSpec(memory_space=pltpu.VMEM)] * 3,
        out_specs=pl.BlockSpec(memory_space=pltpu.VMEM),
        scratch_shapes=[pltpu.VMEM((2, WIN, LANES), jnp.float32)],
        compiler_params=pltpu.CompilerParams(vmem_limit_bytes=16 * MIB),
    )(first, mine, other, inverse)


def vmem_call(kernel, out_shape, scratch, limit, *args):
    return pl.pallas_call(
        kernel,
        out_shape=jax.ShapeDtypeStruct(out_shape, jnp.bfloat16),
        in_specs=[pl.BlockSpec(memory_space=pltpu.VMEM)] * len(args),
        out_specs=pl.BlockSpec(memory_space=pltpu.VMEM),
        scratch_shapes=[pltpu.VMEM(shape, jnp.float32) for shape in scratch],
        compiler_params=pltpu.CompilerParams(vmem_limit_bytes=limit),
    )(*args)


def first_lag_kernel(info, near, inverse, out, wide, held, done, blank, sems):
    bands, step, rows = near.shape[:3]
    depth = bands * step
    table = inverse[...]
    blank[...] = jnp.zeros(blank.shape, jnp.bfloat16)

    def copy(kind, source, act):
        for slot in range(TMAX):

            @pl.when(info[TMAX + slot] == kind)
            def _():
                act(pltpu.make_async_copy(source, out.at[slot], sems.at[slot]))

    copy(2, blank, lambda c: c.start())
    wide[...] = near[...].astype(jnp.float32).reshape(wide.shape)

    def one(pair, carry):
        pieces = [
            wide[pl.ds(2 * pair + k, depth, stride=rows), :].astype(jnp.bfloat16) for k in range(2)
        ]
        result = dot(table, jnp.concatenate(pieces, axis=1), NN)
        for k in range(2):
            value = result[:LAGS, k * LANES : (k + 1) * LANES]
            held[pl.ds(2 * pair + k, LAGS, stride=rows), :] = value
        return carry

    lax.fori_loop(0, rows // 2, one, 0, unroll=True)
    done[...] = held[...].astype(jnp.bfloat16).reshape(done.shape)
    copy(1, done, lambda c: c.start())
    copy(1, done, lambda c: c.wait())
    copy(2, blank, lambda c: c.wait())


def first_lags(info, near, inverse):
    rows = near.shape[2]
    return pl.pallas_call(
        first_lag_kernel,
        out_shape=jax.ShapeDtypeStruct((TMAX, LAGS, rows, LANES), jnp.bfloat16),
        in_specs=[
            pl.BlockSpec(memory_space=pltpu.SMEM),
            pl.BlockSpec(memory_space=pltpu.VMEM),
            pl.BlockSpec(memory_space=pltpu.VMEM),
        ],
        out_specs=pl.BlockSpec(memory_space=pltpu.HBM),
        scratch_shapes=[
            pltpu.VMEM((WIN * rows, LANES), jnp.float32),
            pltpu.VMEM((LAGS * rows, LANES), jnp.float32),
            pltpu.VMEM((LAGS, rows, LANES), jnp.bfloat16),
            pltpu.VMEM((LAGS, rows, LANES), jnp.bfloat16),
            pltpu.SemaphoreType.DMA((TMAX,)),
        ],
        compiler_params=pltpu.CompilerParams(vmem_limit_bytes=16 * MIB),
    )(info, near, inverse)


def lag_kernel(info, begun, same, far, inverse, out, held, parts, done, sems):
    bands, rows, step = far.shape[0], same.shape[0], far.shape[2]
    depth = bands * step
    first = info[2 * TMAX]
    column = lax.broadcasted_iota(jnp.int32, (LAG_ROWS, LANES), 1)
    table = inverse[...]
    reaches = first + rows + RANGE > 3 * CB

    def piece(row):
        return far[:, row].reshape(depth, LANES)

    def paired(row):
        both = dot(table, jnp.concatenate([piece(row), piece(row + 1)], axis=1), NN)
        return both[:, :LANES], both[:, LANES:]

    for unit in range(0, UNITS, 2):
        parts[unit], parts[unit + 1] = paired(rows + unit)
    own_group = (column >= first) & (column < first + GROUP)
    extra = (column >= jnp.where(first == 0, GROUP, 32)) & (column < LOW)
    has_hole = first >= LOW

    def lower(row):
        unit, at = row % UNITS, 32 * (row // UNITS)
        value = parts[unit]
        if at:
            value = pltpu.roll(value, LANES - at, 1)
        turn = jnp.where(has_hole, 32 + LOW + LANES - first, LANES - at + GROUP)
        moved = parts[jnp.where(has_hole, UNITS + row, unit)]
        return jnp.where(extra, pltpu.roll(moved, lax.bitwise_and(turn, LANES - 1), 1), value)

    def put(place, row, value):
        held[place, pl.ds(row, LAGS, stride=rows), :] = value[:LAGS]

    def finish(place, offset):
        done[place] = held[place].astype(jnp.bfloat16).reshape(LAGS, rows, LANES)
        slot = info[offset]

        @pl.when(slot < TMAX)
        def _():
            pltpu.make_async_copy(done.at[place], out.at[slot], sems.at[place]).start()

    def settle(place, offset):
        slot = info[offset]

        @pl.when(slot < TMAX)
        def _():
            pltpu.make_async_copy(done.at[place], out.at[slot], sems.at[place]).wait()

    for pair in range(0, rows, 2):
        for row, shared in zip((pair, pair + 1), paired(pair)):
            parts[UNITS + row] = shared
            put(0, row, jnp.where(column > first + row, shared, 0.0))
    finish(0, 0)
    for row in range(rows):
        i = first + row
        turned = pltpu.roll(parts[UNITS + row], LOW, 1)
        joined = jnp.where(column < LOW, lower(row), turned)
        joined = jnp.where(own_group, same[row], joined)
        put(1, row, jnp.where(column <= i + RANGE - 2 * CB, joined, 0.0))
    finish(1, 2)

    @pl.when(reaches)
    def _():
        for row in range(rows):
            turned = pltpu.roll(parts[UNITS + row], LOW, 1)
            put(2, row, jnp.where(column <= first + row + RANGE - 3 * CB, turned, 0.0))
        finish(2, 3)
        settle(2, 3)

    settle(0, 0)
    settle(1, 2)


def lags(info, begun, same, far, inverse):
    rows = begun.shape[2]
    return pl.pallas_call(
        lag_kernel,
        out_shape=jax.ShapeDtypeStruct(begun.shape, begun.dtype),
        in_specs=[
            pl.BlockSpec(memory_space=pltpu.SMEM),
            pl.BlockSpec(memory_space=pltpu.HBM),
            pl.BlockSpec(memory_space=pltpu.VMEM),
            pl.BlockSpec(memory_space=pltpu.VMEM),
            pl.BlockSpec(memory_space=pltpu.VMEM),
        ],
        out_specs=pl.BlockSpec(memory_space=pltpu.HBM),
        scratch_shapes=[
            pltpu.VMEM((3, LAGS * rows, LANES), jnp.float32),
            pltpu.VMEM((UNITS + rows, LAG_ROWS, LANES), jnp.float32),
            pltpu.VMEM((3, LAGS, rows, LANES), jnp.bfloat16),
            pltpu.SemaphoreType.DMA((3,)),
        ],
        input_output_aliases={1: 0},
        compiler_params=pltpu.CompilerParams(vmem_limit_bytes=32 * MIB),
    )(info, begun, same, far, inverse)


def from_ahead(block, distance, parity=None):
    count = lax.axis_size("chan")
    route = [(i + distance, i) for i in range(count - distance) if parity is None or i % 2 == parity]
    return lax.ppermute(block, "chan", route)


def exchanged(block, axis):
    return lax.all_to_all(block, axis, split_axis=0, concat_axis=0, tiled=True)


def local(traces, window_starts, tile_offsets, tile_count):
    bands = lax.axis_size("band")
    rows = CB // bands
    width = HALF // bands
    forward, inverse = tables(bands)
    series = exchanged(traces, "chan")
    white = whitened_rows(window_starts, series, forward, bands)
    own = exchanged(white, "band")
    next1 = from_ahead(own, 1)
    next2 = (from_ahead(next1, 1, 0), from_ahead(own, 2, 1))
    reach = -(-(RANGE - 2 * CB) // rows)
    next3 = from_ahead(own[:reach], 3)
    near = vmem_call(near_kernel, (bands, 2 * width, rows, LANES), [], 16 * MIB, own, next1)
    near = exchanged(near, "band")
    far = vmem_call(
        far_kernel,
        (bands, rows + UNITS, 2 * width, LANES),
        [
            (CB * 2 * width, LANES),
            (bands * UNITS * 2 * width, LANES),
            (CB * 2 * width, LANES),
        ],
        24 * MIB,
        own,
        *next2,
        next3,
    )
    white, far = lax.optimization_barrier((white, far))
    first = (lax.axis_index("band") * rows).astype(jnp.int32)[None]
    same = local_lags(first, white, from_ahead(white, 2), inverse)
    far = exchanged(far, "band")
    live = jnp.arange(TMAX) < tile_count[0]
    holds = (tile_offsets[0][None, :] == jnp.arange(TMAX)[:, None]) & live[None, :]
    slot_of = jnp.where(holds.any(axis=1), jnp.argmax(holds, axis=1), TMAX)
    reaches = first[0] + rows + RANGE > 3 * CB
    blank = ~live | (holds[3] & ~reaches)
    kind = jnp.where(blank, 2, jnp.where(holds[1], 1, 0))
    info = jnp.concatenate([slot_of, kind, first]).astype(jnp.int32)
    begun = first_lags(info, near, inverse)
    result = lags(info, begun, same, far, inverse)
    return result.transpose(0, 2, 3, 1)[None]


def solution(mesh):
    placed = (P(None, "band", "chan"), P(), P("chan", None), P("chan"))
    return jax.shard_map(
        local,
        mesh=mesh,
        in_specs=placed,
        out_specs=P("chan", None, "band", None, None),
        check_vma=False,
    )
```

```python
import math

import jax
import jax.numpy as jnp
import numpy as np
from jax import lax
from jax.experimental import pallas as pl
from jax.experimental.pallas import tpu as pltpu
from jax.sharding import PartitionSpec as P

CB = 128
RANGE = 300
WIN = 256
HALF = WIN // 2
LAGS = 201
NWIN = 64
TMAX = 4
LANES = 128
LAG_ROWS = 208
PACK = 304
LOW = PACK - 2 * CB
GROUP = 16
UNITS = 4
EPS = 1e-06
MIB = 1 << 20


def tables(bands):
    f32 = np.float32
    turn = f32(2.0 * math.pi)
    times = np.arange(WIN)
    bins = np.arange(HALF)
    hann = f32(0.5) - f32(0.5) * np.cos(turn * times.astype(f32) / f32(WIN))
    phase = turn * (times[:, None] * bins[None, :] % WIN).astype(f32) / f32(WIN)
    forward = np.concatenate([hann[:, None] * np.cos(phase), -hann[:, None] * np.sin(phase)], axis=1)
    shifts = np.arange(LAGS) - (LAGS - 1) // 2
    angle = turn * (bins[:, None] * shifts[None, :] % WIN).astype(f32) / f32(WIN)
    factor = np.where(bins == 0, 1.0, 2.0).astype(f32)[:, None]
    inverse = np.stack([factor * np.cos(angle), -factor * np.sin(angle)], axis=0)
    width = HALF // bands
    inverse = inverse.reshape(2, bands, width, LAGS).transpose(1, 0, 2, 3).reshape(WIN, LAGS)
    inverse = np.pad(inverse.T, ((0, LAG_ROWS - LAGS), (0, 0)))
    return (
        jnp.asarray(forward.T.astype(jnp.bfloat16)),
        jnp.asarray(inverse.astype(jnp.bfloat16)),
    )


NT = (((1,), (1,)), ((), ()))
NN = (((1,), (0,)), ((), ()))


def dot(a, b, dims):
    return lax.dot_general(a, b, dims, preferred_element_type=jnp.float32)


def spectra_kernel(starts, traces, forward, out, seg0, seg1, white):
    rows, samples = traces.shape[1], traces.shape[2]
    log_lanes = LANES.bit_length() - 1
    chunks = samples // LANES
    log_chunks = chunks.bit_length() - 1
    last = traces.shape[0] * chunks - 1
    lane = lax.broadcasted_iota(jnp.int32, (rows, LANES), 1)

    def cut(w, carry):
        begin = starts[w]
        first = lax.shift_right_logical(begin, log_lanes)
        shift = lax.bitwise_and(begin, LANES - 1)
        turn = lax.bitwise_and(LANES - shift, LANES - 1)

        def chunk(index):
            at = pl.multiple_of(lax.bitwise_and(index, chunks - 1) * LANES, LANES)
            shard = lax.shift_right_logical(index, log_chunks)
            piece = traces[shard, :, pl.ds(at, LANES)].astype(jnp.float32)
            return pltpu.roll(piece, turn, 1)

        a, b, c = chunk(first), chunk(first + 1), chunk(jnp.minimum(first + 2, last))
        inside = lane < LANES - shift
        seg0[pl.ds(w, rows, stride=NWIN), :] = jnp.where(inside, a, b)
        seg1[pl.ds(w, rows, stride=NWIN), :] = jnp.where(inside, b, c)
        return carry

    lax.fori_loop(0, NWIN, cut, 0, unroll=True)
    real_lane = lax.broadcasted_iota(jnp.int32, (HALF, 2 * LANES), 1) % LANES < NWIN

    def transform(pair, carry):
        at = pl.multiple_of(pair * LANES, LANES)
        both = jnp.concatenate([seg0[pl.ds(at, LANES), :], seg1[pl.ds(at, LANES), :]], axis=1)
        both = both.astype(jnp.bfloat16).reshape(2, NWIN, WIN)
        twice = jnp.concatenate([both, both], axis=1).reshape(4 * NWIN, WIN)
        result = dot(forward[...], twice, NT)
        spectra = jnp.where(real_lane, result[:HALF], result[HALF:])
        spectra = spectra.astype(jnp.bfloat16).astype(jnp.float32)
        for half in range(2):
            mine = spectra[:, half * LANES : (half + 1) * LANES]
            power = jnp.sum(mine * mine, axis=1, keepdims=True) * (1.0 / NWIN)
            white[pl.ds(2 * pair + half, HALF, stride=rows), :] = mine * lax.rsqrt(power + EPS)
        return carry

    lax.fori_loop(0, rows // 2, transform, 0, unroll=True)
    out[...] = white[: HALF * rows].astype(jnp.bfloat16).reshape(out.shape)


def whitened_rows(starts, series, forward, bands):
    rows = series.shape[1]
    width = HALF // bands
    return pl.pallas_call(
        spectra_kernel,
        out_shape=jax.ShapeDtypeStruct((bands, width, rows, LANES), jnp.bfloat16),
        in_specs=[
            pl.BlockSpec(memory_space=pltpu.SMEM),
            pl.BlockSpec(memory_space=pltpu.VMEM),
            pl.BlockSpec(memory_space=pltpu.VMEM),
        ],
        out_specs=pl.BlockSpec(memory_space=pltpu.VMEM),
        scratch_shapes=[
            pltpu.VMEM(((rows + 1) * NWIN, LANES), jnp.float32),
            pltpu.VMEM(((rows + 1) * NWIN, LANES), jnp.float32),
            pltpu.VMEM(((HALF + 1) * rows, LANES), jnp.float32),
        ],
        compiler_params=pltpu.CompilerParams(vmem_limit_bytes=16 * MIB),
    )(starts, series, forward)


def both_sides(own, f):
    mine = own[:, f].reshape(CB, LANES)
    wide = mine.astype(jnp.float32)
    lane = lax.broadcasted_iota(jnp.int32, (CB, LANES), 1)
    turned = pltpu.roll(wide, NWIN, 1)
    turned = jnp.where(lane < NWIN, -turned, turned).astype(jnp.bfloat16)
    return mine, jnp.concatenate([mine, turned], axis=0)


def near_kernel(own, next1, out):
    bands, width, rows = own.shape[:3]

    def one(f, carry):
        mine, sides = both_sides(own, f)
        result = dot(sides, next1[:, f].reshape(CB, LANES), NT) * (1.0 / NWIN)
        result = result.astype(jnp.bfloat16).reshape(2, bands, rows, LANES)
        out[:, f] = result[0]
        out[:, width + f] = result[1]
        return carry

    lax.fori_loop(0, width, one, 0, unroll=True)


def far_kernel(own, next2_even, next2_odd, next3, out, held0, held1, plain):
    bands, width, rows = own.shape[:3]
    step = 2 * width
    row_index = lax.broadcasted_iota(jnp.int32, (CB, LANES), 0)
    column = lax.broadcasted_iota(jnp.int32, (CB, LANES), 1)
    after = column > row_index
    band = row_index // GROUP
    hole = column // GROUP == band - LOW // GROUP
    second_half = column // GROUP % 2 == 1
    lane = lax.broadcasted_iota(jnp.int32, (bands, LANES), 1)

    def one(f, carry):
        mine, sides = both_sides(own, f)
        second = (next2_even[:, f] + next2_odd[:, f]).reshape(CB, LANES)
        third = next3[:, f].reshape(LOW, LANES)
        copies = LANES // GROUP
        low = [second[k * GROUP : (k + 1) * GROUP] for k in range(3) for _ in range(copies)]
        mixed = jnp.concatenate([mine, second[LOW:], third] + low, axis=0)
        result = dot(sides, mixed, NT) * (1.0 / NWIN)
        for part in range(2):
            of = result[part * CB : (part + 1) * CB]
            at = part * width + f
            here, there, low0, low1, low2 = (of[:, k * CB : (k + 1) * CB] for k in range(5))
            shared = jnp.where(hole, low2, jnp.where(after, here, there))
            held0[pl.ds(at, CB, stride=step), :] = shared
            left = jnp.where(band == 0, low1, low0)
            right = jnp.where(band <= 1, low2, low1)
            base = at * CB
            plain[pl.ds(base, CB), :] = jnp.where(second_half, right, left)
            for unit in range(UNITS):
                value = plain[pl.ds(base + unit + 12, bands, stride=rows), :]
                for k in (2, 1, 0):
                    other = plain[pl.ds(base + unit + 4 * k, bands, stride=rows), :]
                    value = jnp.where(lane < 32 * (k + 1), other, value)
                held1[pl.ds(unit * step + at, bands, stride=UNITS * step), :] = value
        return carry

    lax.fori_loop(0, width, one, 0, unroll=True)
    out[:, :rows] = held0[: CB * step].astype(jnp.bfloat16).reshape(bands, rows, step, LANES)
    out[:, rows:] = held1[: bands * UNITS * step].astype(jnp.bfloat16).reshape(bands, UNITS, step, LANES)


def local_kernel(first, mine, other, inverse, out, held):
    bands, width, rows = mine.shape[:3]
    copies = LANES // GROUP
    lane = lax.broadcasted_iota(jnp.int32, (rows, LANES), 1)
    row_index = lax.broadcasted_iota(jnp.int32, (rows, LANES), 0)
    wanted = lane // GROUP == row_index % copies

    def one(f, carry):
        for band in range(bands):
            rows_of = mine[band, f]
            wide = rows_of.astype(jnp.float32)
            turned = pltpu.roll(wide, NWIN, 1)
            turned = jnp.where(lane < NWIN, -turned, turned).astype(jnp.bfloat16)
            sides = jnp.concatenate([rows_of, turned], axis=0)
            columns = jnp.concatenate([other[band, f]] * copies, axis=0)
            result = dot(sides, columns, NT) * (1.0 / NWIN)
            for part in range(2):
                picked = jnp.where(wanted, result[part * rows : (part + 1) * rows], 0.0)
                for half in range(2):
                    line = jnp.sum(picked[half * copies : (half + 1) * copies], axis=0, keepdims=True)
                    held[half, pl.ds(band * 2 * width + part * width + f, 1), :] = line
        return carry

    lax.fori_loop(0, width, one, 0)
    for half in range(2):
        result = dot(inverse[...], held[half].astype(jnp.bfloat16), NN)
        for k in range(copies):
            turn = lax.bitwise_and(first[0] + (LANES - GROUP * k), LANES - 1)
            out[half * copies + k] = pltpu.roll(result, turn, 1)


def local_lags(first, mine, other, inverse):
    return pl.pallas_call(
        local_kernel,
        out_shape=jax.ShapeDtypeStruct((mine.shape[2], LAG_ROWS, LANES), jnp.float32),
        in_specs=[pl.BlockSpec(memory_space=pltpu.SMEM)]
        + [pl.BlockSpec(memory_space=pltpu.VMEM)] * 3,
        out_specs=pl.BlockSpec(memory_space=pltpu.VMEM),
        scratch_shapes=[pltpu.VMEM((2, WIN, LANES), jnp.float32)],
        compiler_params=pltpu.CompilerParams(vmem_limit_bytes=16 * MIB),
    )(first, mine, other, inverse)


def vmem_call(kernel, out_shape, scratch, limit, *args):
    return pl.pallas_call(
        kernel,
        out_shape=jax.ShapeDtypeStruct(out_shape, jnp.bfloat16),
        in_specs=[pl.BlockSpec(memory_space=pltpu.VMEM)] * len(args),
        out_specs=pl.BlockSpec(memory_space=pltpu.VMEM),
        scratch_shapes=[pltpu.VMEM(shape, jnp.float32) for shape in scratch],
        compiler_params=pltpu.CompilerParams(vmem_limit_bytes=limit),
    )(*args)


def first_lag_kernel(info, near, inverse, out, wide, held, done, blank, sems):
    bands, step, rows = near.shape[:3]
    depth = bands * step
    table = inverse[...]
    blank[...] = jnp.zeros(blank.shape, jnp.bfloat16)

    def copy(kind, source, act):
        for slot in range(TMAX):

            @pl.when(info[TMAX + slot] == kind)
            def _():
                act(pltpu.make_async_copy(source, out.at[slot], sems.at[slot]))

    copy(2, blank, lambda c: c.start())
    wide[: depth * rows] = near[...].astype(jnp.float32).reshape(depth * rows, LANES)

    def one(pair, carry):
        pieces = [
            wide[pl.ds(2 * pair + k, depth, stride=rows), :].astype(jnp.bfloat16) for k in range(2)
        ]
        result = dot(table, jnp.concatenate(pieces, axis=1), NN)
        for k in range(2):
            value = result[:LAGS, k * LANES : (k + 1) * LANES]
            held[pl.ds(2 * pair + k, LAGS, stride=rows), :] = value
        return carry

    lax.fori_loop(0, rows // 2, one, 0, unroll=True)
    done[...] = held[: LAGS * rows].astype(jnp.bfloat16).reshape(done.shape)
    copy(1, done, lambda c: c.start())
    copy(1, done, lambda c: c.wait())
    copy(2, blank, lambda c: c.wait())


def first_lags(info, near, inverse):
    rows = near.shape[2]
    return pl.pallas_call(
        first_lag_kernel,
        out_shape=jax.ShapeDtypeStruct((TMAX, LAGS, rows, LANES), jnp.bfloat16),
        in_specs=[
            pl.BlockSpec(memory_space=pltpu.SMEM),
            pl.BlockSpec(memory_space=pltpu.VMEM),
            pl.BlockSpec(memory_space=pltpu.VMEM),
        ],
        out_specs=pl.BlockSpec(memory_space=pltpu.HBM),
        scratch_shapes=[
            pltpu.VMEM(((WIN + 1) * rows, LANES), jnp.float32),
            pltpu.VMEM(((LAGS + 1) * rows, LANES), jnp.float32),
            pltpu.VMEM((LAGS, rows, LANES), jnp.bfloat16),
            pltpu.VMEM((LAGS, rows, LANES), jnp.bfloat16),
            pltpu.SemaphoreType.DMA((TMAX,)),
        ],
        compiler_params=pltpu.CompilerParams(vmem_limit_bytes=16 * MIB),
    )(info, near, inverse)


def lag_kernel(info, begun, same, far, inverse, out, held, parts, done, sems):
    bands, rows, step = far.shape[0], same.shape[0], far.shape[2]
    depth = bands * step
    first = info[2 * TMAX]
    column = lax.broadcasted_iota(jnp.int32, (LAG_ROWS, LANES), 1)
    table = inverse[...]
    reaches = first + rows + RANGE > 3 * CB

    def piece(row):
        return far[:, row].reshape(depth, LANES)

    def paired(row):
        both = dot(table, jnp.concatenate([piece(row), piece(row + 1)], axis=1), NN)
        return both[:, :LANES], both[:, LANES:]

    for unit in range(0, UNITS, 2):
        parts[unit], parts[unit + 1] = paired(rows + unit)
    own_group = (column >= first) & (column < first + GROUP)
    extra = (column >= jnp.where(first == 0, GROUP, 32)) & (column < LOW)
    has_hole = first >= LOW

    def lower(row):
        unit, at = row % UNITS, 32 * (row // UNITS)
        value = parts[unit]
        if at:
            value = pltpu.roll(value, LANES - at, 1)
        turn = jnp.where(has_hole, 32 + LOW + LANES - first, LANES - at + GROUP)
        moved = parts[jnp.where(has_hole, UNITS + row, unit)]
        return jnp.where(extra, pltpu.roll(moved, lax.bitwise_and(turn, LANES - 1), 1), value)

    def put(place, row, value):
        held[place, pl.ds(row, LAGS, stride=rows), :] = value[:LAGS]

    def finish(place, offset):
        values = held[place, : LAGS * rows]
        done[place] = values.astype(jnp.bfloat16).reshape(LAGS, rows, LANES)
        slot = info[offset]

        @pl.when(slot < TMAX)
        def _():
            pltpu.make_async_copy(done.at[place], out.at[slot], sems.at[place]).start()

    def settle(place, offset):
        slot = info[offset]

        @pl.when(slot < TMAX)
        def _():
            pltpu.make_async_copy(done.at[place], out.at[slot], sems.at[place]).wait()

    for pair in range(0, rows, 2):
        for row, shared in zip((pair, pair + 1), paired(pair)):
            parts[UNITS + row] = shared
            put(0, row, jnp.where(column > first + row, shared, 0.0))
    finish(0, 0)
    for row in range(rows):
        i = first + row
        turned = pltpu.roll(parts[UNITS + row], LOW, 1)
        joined = jnp.where(column < LOW, lower(row), turned)
        joined = jnp.where(own_group, same[row], joined)
        put(1, row, jnp.where(column <= i + RANGE - 2 * CB, joined, 0.0))
    finish(1, 2)

    @pl.when(reaches)
    def _():
        for row in range(rows):
            turned = pltpu.roll(parts[UNITS + row], LOW, 1)
            put(2, row, jnp.where(column <= first + row + RANGE - 3 * CB, turned, 0.0))
        finish(2, 3)
        settle(2, 3)

    settle(0, 0)
    settle(1, 2)


def lags(info, begun, same, far, inverse):
    rows = begun.shape[2]
    return pl.pallas_call(
        lag_kernel,
        out_shape=jax.ShapeDtypeStruct(begun.shape, begun.dtype),
        in_specs=[
            pl.BlockSpec(memory_space=pltpu.SMEM),
            pl.BlockSpec(memory_space=pltpu.HBM),
            pl.BlockSpec(memory_space=pltpu.VMEM),
            pl.BlockSpec(memory_space=pltpu.VMEM),
            pl.BlockSpec(memory_space=pltpu.VMEM),
        ],
        out_specs=pl.BlockSpec(memory_space=pltpu.HBM),
        scratch_shapes=[
            pltpu.VMEM((3, (LAGS + 1) * rows, LANES), jnp.float32),
            pltpu.VMEM((UNITS + rows, LAG_ROWS, LANES), jnp.float32),
            pltpu.VMEM((3, LAGS, rows, LANES), jnp.bfloat16),
            pltpu.SemaphoreType.DMA((3,)),
        ],
        input_output_aliases={1: 0},
        compiler_params=pltpu.CompilerParams(vmem_limit_bytes=32 * MIB),
    )(info, begun, same, far, inverse)


def from_ahead(block, distance, parity=None):
    count = lax.axis_size("chan")
    route = [(i + distance, i) for i in range(count - distance) if parity is None or i % 2 == parity]
    return lax.ppermute(block, "chan", route)


def exchanged(block, axis):
    return lax.all_to_all(block, axis, split_axis=0, concat_axis=0, tiled=True)


def local(traces, window_starts, tile_offsets, tile_count):
    bands = lax.axis_size("band")
    rows = CB // bands
    width = HALF // bands
    forward, inverse = tables(bands)
    series = exchanged(traces, "chan")
    white = whitened_rows(window_starts, series, forward, bands)
    own = exchanged(white, "band")
    next1 = from_ahead(own, 1)
    next2 = (from_ahead(next1, 1, 0), from_ahead(own, 2, 1))
    reach = -(-(RANGE - 2 * CB) // rows)
    next3 = from_ahead(own[:reach], 3)
    near = vmem_call(near_kernel, (bands, 2 * width, rows, LANES), [], 16 * MIB, own, next1)
    near = exchanged(near, "band")
    far = vmem_call(
        far_kernel,
        (bands, rows + UNITS, 2 * width, LANES),
        [
            ((CB + 1) * 2 * width, LANES),
            ((bands + 1) * UNITS * 2 * width, LANES),
            ((CB + 1) * 2 * width, LANES),
        ],
        24 * MIB,
        own,
        *next2,
        next3,
    )
    white, far = lax.optimization_barrier((white, far))
    first = (lax.axis_index("band") * rows).astype(jnp.int32)[None]
    same = local_lags(first, white, from_ahead(white, 2), inverse)
    far = exchanged(far, "band")
    live = jnp.arange(TMAX) < tile_count[0]
    holds = (tile_offsets[0][None, :] == jnp.arange(TMAX)[:, None]) & live[None, :]
    slot_of = jnp.where(holds.any(axis=1), jnp.argmax(holds, axis=1), TMAX)
    reaches = first[0] + rows + RANGE > 3 * CB
    blank = ~live | (holds[3] & ~reaches)
    kind = jnp.where(blank, 2, jnp.where(holds[1], 1, 0))
    info = jnp.concatenate([slot_of, kind, first]).astype(jnp.int32)
    begun = first_lags(info, near, inverse)
    result = lags(info, begun, same, far, inverse)
    return result.transpose(0, 2, 3, 1)[None]


def solution(mesh):
    placed = (P(None, "band", "chan"), P(), P("chan", None), P("chan"))
    return jax.shard_map(
        local,
        mesh=mesh,
        in_specs=placed,
        out_specs=P("chan", None, "band", None, None),
        check_vma=False,
    )
```

```python
import math

import jax
import jax.numpy as jnp
import numpy as np
from jax import lax
from jax.experimental import pallas as pl
from jax.experimental.pallas import tpu as pltpu
from jax.sharding import PartitionSpec as P

CB = 128
RANGE = 300
WIN = 256
HALF = WIN // 2
LAGS = 201
NWIN = 64
TMAX = 4
LANES = 128
LAG_ROWS = 208
PACK = 304
LOW = PACK - 2 * CB
GROUP = 16
UNITS = 4
EPS = 1e-06
MIB = 1 << 20


def tables(bands):
    f32 = np.float32
    turn = f32(2.0 * math.pi)
    times = np.arange(WIN)
    bins = np.arange(HALF)
    hann = f32(0.5) - f32(0.5) * np.cos(turn * times.astype(f32) / f32(WIN))
    phase = turn * (times[:, None] * bins[None, :] % WIN).astype(f32) / f32(WIN)
    forward = np.concatenate([hann[:, None] * np.cos(phase), -hann[:, None] * np.sin(phase)], axis=1)
    shifts = np.arange(LAGS) - (LAGS - 1) // 2
    angle = turn * (bins[:, None] * shifts[None, :] % WIN).astype(f32) / f32(WIN)
    factor = np.where(bins == 0, 1.0, 2.0).astype(f32)[:, None]
    inverse = np.stack([factor * np.cos(angle), -factor * np.sin(angle)], axis=0)
    width = HALF // bands
    inverse = inverse.reshape(2, bands, width, LAGS).transpose(1, 0, 2, 3).reshape(WIN, LAGS)
    inverse = np.pad(inverse.T, ((0, LAG_ROWS - LAGS), (0, 0)))
    return (
        jnp.asarray(forward.T.astype(jnp.bfloat16)),
        jnp.asarray(inverse.astype(jnp.bfloat16)),
    )


NT = (((1,), (1,)), ((), ()))
NN = (((1,), (0,)), ((), ()))


def dot(a, b, dims):
    return lax.dot_general(a, b, dims, preferred_element_type=jnp.float32)


def spectra_kernel(starts, traces, forward, out, seg0, seg1, white):
    rows, samples = traces.shape[1], traces.shape[2]
    log_lanes = LANES.bit_length() - 1
    chunks = samples // LANES
    log_chunks = chunks.bit_length() - 1
    last = traces.shape[0] * chunks - 1
    lane = lax.broadcasted_iota(jnp.int32, (rows, LANES), 1)

    def cut(w, carry):
        begin = starts[w]
        first = lax.shift_right_logical(begin, log_lanes)
        shift = lax.bitwise_and(begin, LANES - 1)
        turn = lax.bitwise_and(LANES - shift, LANES - 1)

        def chunk(index):
            at = pl.multiple_of(lax.bitwise_and(index, chunks - 1) * LANES, LANES)
            shard = lax.shift_right_logical(index, log_chunks)
            piece = traces[shard, :, pl.ds(at, LANES)].astype(jnp.float32)
            return pltpu.roll(piece, turn, 1)

        a, b, c = chunk(first), chunk(first + 1), chunk(jnp.minimum(first + 2, last))
        inside = lane < LANES - shift
        seg0[pl.ds(w, rows, stride=NWIN), :] = jnp.where(inside, a, b)
        seg1[pl.ds(w, rows, stride=NWIN), :] = jnp.where(inside, b, c)
        return carry

    lax.fori_loop(0, NWIN, cut, 0, unroll=True)
    real_lane = lax.broadcasted_iota(jnp.int32, (HALF, 2 * LANES), 1) % LANES < NWIN

    def transform(pair, carry):
        at = pl.multiple_of(pair * LANES, LANES)
        both = jnp.concatenate([seg0[pl.ds(at, LANES), :], seg1[pl.ds(at, LANES), :]], axis=1)
        both = both.astype(jnp.bfloat16).reshape(2, NWIN, WIN)
        twice = jnp.concatenate([both, both], axis=1).reshape(4 * NWIN, WIN)
        result = dot(forward[...], twice, NT)
        spectra = jnp.where(real_lane, result[:HALF], result[HALF:])
        spectra = spectra.astype(jnp.bfloat16).astype(jnp.float32)
        for half in range(2):
            mine = spectra[:, half * LANES : (half + 1) * LANES]
            power = jnp.sum(mine * mine, axis=1, keepdims=True) * (1.0 / NWIN)
            white[pl.ds(2 * pair + half, HALF, stride=rows), :] = mine * lax.rsqrt(power + EPS)
        return carry

    lax.fori_loop(0, rows // 2, transform, 0, unroll=True)
    out[...] = white[: HALF * rows].astype(jnp.bfloat16).reshape(out.shape)


def whitened_rows(starts, series, forward, bands):
    rows = series.shape[1]
    width = HALF // bands
    return pl.pallas_call(
        spectra_kernel,
        out_shape=jax.ShapeDtypeStruct((bands, width, rows, LANES), jnp.bfloat16),
        in_specs=[
            pl.BlockSpec(memory_space=pltpu.SMEM),
            pl.BlockSpec(memory_space=pltpu.VMEM),
            pl.BlockSpec(memory_space=pltpu.VMEM),
        ],
        out_specs=pl.BlockSpec(memory_space=pltpu.VMEM),
        scratch_shapes=[
            pltpu.VMEM(((rows + 1) * NWIN, LANES), jnp.float32),
            pltpu.VMEM(((rows + 1) * NWIN, LANES), jnp.float32),
            pltpu.VMEM(((HALF + 1) * rows, LANES), jnp.float32),
        ],
        compiler_params=pltpu.CompilerParams(vmem_limit_bytes=16 * MIB),
    )(starts, series, forward)


def both_sides(own, f):
    mine = own[:, f].reshape(own.shape[0] * own.shape[2], LANES)
    wide = mine.astype(jnp.float32)
    lane = lax.broadcasted_iota(jnp.int32, mine.shape, 1)
    turned = pltpu.roll(wide, NWIN, 1)
    turned = jnp.where(lane < NWIN, -turned, turned).astype(jnp.bfloat16)
    return mine, jnp.concatenate([mine, turned], axis=0)


def near_kernel(own, next1, out):
    bands, width, rows = own.shape[:3]

    def one(f, carry):
        mine, sides = both_sides(own, f)
        result = dot(sides, next1[:, f].reshape(CB, LANES), NT) * (1.0 / NWIN)
        result = result.astype(jnp.bfloat16).reshape(2, bands, rows, LANES)
        out[:, f] = result[0]
        out[:, width + f] = result[1]
        return carry

    lax.fori_loop(0, width, one, 0, unroll=True)


def near_cross(own, next1):
    bands, width, rows = own.shape[:3]
    part = bands // 2
    return pl.pallas_call(
        near_kernel,
        out_shape=jax.ShapeDtypeStruct((bands, 2 * width, rows, LANES), jnp.bfloat16),
        grid=(2,),
        in_specs=[
            pl.BlockSpec((part, width, rows, LANES), lambda g: (g, 0, 0, 0)),
            pl.BlockSpec(own.shape, lambda g: (0, 0, 0, 0)),
        ],
        out_specs=pl.BlockSpec((part, 2 * width, rows, LANES), lambda g: (g, 0, 0, 0)),
        compiler_params=pltpu.CompilerParams(vmem_limit_bytes=16 * MIB),
    )(own, next1)


def far_kernel(own, next2_even, next2_odd, next3, out, held0, held1, plain):
    bands, width, rows = own.shape[:3]
    step = 2 * width
    row_index = lax.broadcasted_iota(jnp.int32, (CB, LANES), 0)
    column = lax.broadcasted_iota(jnp.int32, (CB, LANES), 1)
    after = column > row_index
    band = row_index // GROUP
    hole = column // GROUP == band - LOW // GROUP
    second_half = column // GROUP % 2 == 1
    lane = lax.broadcasted_iota(jnp.int32, (bands, LANES), 1)

    def one(f, carry):
        mine, sides = both_sides(own, f)
        second = (next2_even[:, f] + next2_odd[:, f]).reshape(CB, LANES)
        third = next3[:, f].reshape(LOW, LANES)
        copies = LANES // GROUP
        low = [second[k * GROUP : (k + 1) * GROUP] for k in range(3) for _ in range(copies)]
        mixed = jnp.concatenate([mine, second[LOW:], third] + low, axis=0)
        result = dot(sides, mixed, NT) * (1.0 / NWIN)
        for part in range(2):
            of = result[part * CB : (part + 1) * CB]
            at = part * width + f
            here, there, low0, low1, low2 = (of[:, k * CB : (k + 1) * CB] for k in range(5))
            shared = jnp.where(hole, low2, jnp.where(after, here, there))
            held0[pl.ds(at, CB, stride=step), :] = shared
            left = jnp.where(band == 0, low1, low0)
            right = jnp.where(band <= 1, low2, low1)
            base = at * CB
            plain[pl.ds(base, CB), :] = jnp.where(second_half, right, left)
            for unit in range(UNITS):
                value = plain[pl.ds(base + unit + 12, bands, stride=rows), :]
                for k in (2, 1, 0):
                    other = plain[pl.ds(base + unit + 4 * k, bands, stride=rows), :]
                    value = jnp.where(lane < 32 * (k + 1), other, value)
                held1[pl.ds(unit * step + at, bands, stride=UNITS * step), :] = value
        return carry

    lax.fori_loop(0, width, one, 0, unroll=True)
    out[:, :rows] = held0[: CB * step].astype(jnp.bfloat16).reshape(bands, rows, step, LANES)
    out[:, rows:] = held1[: bands * UNITS * step].astype(jnp.bfloat16).reshape(bands, UNITS, step, LANES)


def local_kernel(first, mine, other, inverse, out, held):
    bands, width, rows = mine.shape[:3]
    copies = LANES // GROUP
    lane = lax.broadcasted_iota(jnp.int32, (rows, LANES), 1)
    row_index = lax.broadcasted_iota(jnp.int32, (rows, LANES), 0)
    wanted = lane // GROUP == row_index % copies

    def one(f, carry):
        for band in range(bands):
            rows_of = mine[band, f]
            wide = rows_of.astype(jnp.float32)
            turned = pltpu.roll(wide, NWIN, 1)
            turned = jnp.where(lane < NWIN, -turned, turned).astype(jnp.bfloat16)
            sides = jnp.concatenate([rows_of, turned], axis=0)
            columns = jnp.concatenate([other[band, f]] * copies, axis=0)
            result = dot(sides, columns, NT) * (1.0 / NWIN)
            for part in range(2):
                picked = jnp.where(wanted, result[part * rows : (part + 1) * rows], 0.0)
                for half in range(2):
                    line = jnp.sum(picked[half * copies : (half + 1) * copies], axis=0, keepdims=True)
                    held[half, pl.ds(band * 2 * width + part * width + f, 1), :] = line
        return carry

    lax.fori_loop(0, width, one, 0)
    for half in range(2):
        result = dot(inverse[...], held[half].astype(jnp.bfloat16), NN)
        for k in range(copies):
            turn = lax.bitwise_and(first[0] + (LANES - GROUP * k), LANES - 1)
            out[half * copies + k] = pltpu.roll(result, turn, 1)


def local_lags(first, mine, other, inverse):
    return pl.pallas_call(
        local_kernel,
        out_shape=jax.ShapeDtypeStruct((mine.shape[2], LAG_ROWS, LANES), jnp.float32),
        in_specs=[pl.BlockSpec(memory_space=pltpu.SMEM)]
        + [pl.BlockSpec(memory_space=pltpu.VMEM)] * 3,
        out_specs=pl.BlockSpec(memory_space=pltpu.VMEM),
        scratch_shapes=[pltpu.VMEM((2, WIN, LANES), jnp.float32)],
        compiler_params=pltpu.CompilerParams(vmem_limit_bytes=16 * MIB),
    )(first, mine, other, inverse)


def vmem_call(kernel, out_shape, scratch, limit, *args):
    return pl.pallas_call(
        kernel,
        out_shape=jax.ShapeDtypeStruct(out_shape, jnp.bfloat16),
        in_specs=[pl.BlockSpec(memory_space=pltpu.VMEM)] * len(args),
        out_specs=pl.BlockSpec(memory_space=pltpu.VMEM),
        scratch_shapes=[pltpu.VMEM(shape, jnp.float32) for shape in scratch],
        compiler_params=pltpu.CompilerParams(vmem_limit_bytes=limit),
    )(*args)


def first_lag_kernel(info, near, inverse, out, wide, held, done, blank, sems):
    bands, step, rows = near.shape[:3]
    depth = bands * step
    table = inverse[...]
    blank[...] = jnp.zeros(blank.shape, jnp.bfloat16)

    def copy(kind, source, act):
        for slot in range(TMAX):

            @pl.when(info[TMAX + slot] == kind)
            def _():
                act(pltpu.make_async_copy(source, out.at[slot], sems.at[slot]))

    copy(2, blank, lambda c: c.start())
    wide[: depth * rows] = near[...].astype(jnp.float32).reshape(depth * rows, LANES)

    def one(pair, carry):
        pieces = [
            wide[pl.ds(2 * pair + k, depth, stride=rows), :].astype(jnp.bfloat16) for k in range(2)
        ]
        result = dot(table, jnp.concatenate(pieces, axis=1), NN)
        for k in range(2):
            value = result[:LAGS, k * LANES : (k + 1) * LANES]
            held[pl.ds(2 * pair + k, LAGS, stride=rows), :] = value
        return carry

    lax.fori_loop(0, rows // 2, one, 0, unroll=True)
    done[...] = held[: LAGS * rows].astype(jnp.bfloat16).reshape(done.shape)
    copy(1, done, lambda c: c.start())
    copy(1, done, lambda c: c.wait())
    copy(2, blank, lambda c: c.wait())


def first_lags(info, near, inverse):
    rows = near.shape[2]
    return pl.pallas_call(
        first_lag_kernel,
        out_shape=jax.ShapeDtypeStruct((TMAX, LAGS, rows, LANES), jnp.bfloat16),
        in_specs=[
            pl.BlockSpec(memory_space=pltpu.SMEM),
            pl.BlockSpec(memory_space=pltpu.VMEM),
            pl.BlockSpec(memory_space=pltpu.VMEM),
        ],
        out_specs=pl.BlockSpec(memory_space=pltpu.HBM),
        scratch_shapes=[
            pltpu.VMEM(((WIN + 1) * rows, LANES), jnp.float32),
            pltpu.VMEM(((LAGS + 1) * rows, LANES), jnp.float32),
            pltpu.VMEM((LAGS, rows, LANES), jnp.bfloat16),
            pltpu.VMEM((LAGS, rows, LANES), jnp.bfloat16),
            pltpu.SemaphoreType.DMA((TMAX,)),
        ],
        compiler_params=pltpu.CompilerParams(vmem_limit_bytes=16 * MIB),
    )(info, near, inverse)


def lag_kernel(info, begun, same, far, inverse, out, held, parts, done, sems):
    bands, rows, step = far.shape[0], same.shape[0], far.shape[2]
    depth = bands * step
    first = info[2 * TMAX]
    column = lax.broadcasted_iota(jnp.int32, (LAG_ROWS, LANES), 1)
    table = inverse[...]
    reaches = first + rows + RANGE > 3 * CB

    def piece(row):
        return far[:, row].reshape(depth, LANES)

    def paired(row):
        both = dot(table, jnp.concatenate([piece(row), piece(row + 1)], axis=1), NN)
        return both[:, :LANES], both[:, LANES:]

    for unit in range(0, UNITS, 2):
        parts[unit], parts[unit + 1] = paired(rows + unit)
    own_group = (column >= first) & (column < first + GROUP)
    extra = (column >= jnp.where(first == 0, GROUP, 32)) & (column < LOW)
    has_hole = first >= LOW

    def lower(row):
        unit, at = row % UNITS, 32 * (row // UNITS)
        value = parts[unit]
        if at:
            value = pltpu.roll(value, LANES - at, 1)
        turn = jnp.where(has_hole, 32 + LOW + LANES - first, LANES - at + GROUP)
        moved = parts[jnp.where(has_hole, UNITS + row, unit)]
        return jnp.where(extra, pltpu.roll(moved, lax.bitwise_and(turn, LANES - 1), 1), value)

    def put(place, row, value):
        held[place, pl.ds(row, LAGS, stride=rows), :] = value[:LAGS]

    def finish(place, offset):
        values = held[place, : LAGS * rows]
        done[place] = values.astype(jnp.bfloat16).reshape(LAGS, rows, LANES)
        slot = info[offset]

        @pl.when(slot < TMAX)
        def _():
            pltpu.make_async_copy(done.at[place], out.at[slot], sems.at[place]).start()

    def settle(place, offset):
        slot = info[offset]

        @pl.when(slot < TMAX)
        def _():
            pltpu.make_async_copy(done.at[place], out.at[slot], sems.at[place]).wait()

    for pair in range(0, rows, 2):
        for row, shared in zip((pair, pair + 1), paired(pair)):
            parts[UNITS + row] = shared
            put(0, row, jnp.where(column > first + row, shared, 0.0))
    finish(0, 0)
    for row in range(rows):
        i = first + row
        turned = pltpu.roll(parts[UNITS + row], LOW, 1)
        joined = jnp.where(column < LOW, lower(row), turned)
        joined = jnp.where(own_group, same[row], joined)
        put(1, row, jnp.where(column <= i + RANGE - 2 * CB, joined, 0.0))
    finish(1, 2)

    @pl.when(reaches)
    def _():
        for row in range(rows):
            turned = pltpu.roll(parts[UNITS + row], LOW, 1)
            put(2, row, jnp.where(column <= first + row + RANGE - 3 * CB, turned, 0.0))
        finish(2, 3)
        settle(2, 3)

    settle(0, 0)
    settle(1, 2)


def lags(info, begun, same, far, inverse):
    rows = begun.shape[2]
    return pl.pallas_call(
        lag_kernel,
        out_shape=jax.ShapeDtypeStruct(begun.shape, begun.dtype),
        in_specs=[
            pl.BlockSpec(memory_space=pltpu.SMEM),
            pl.BlockSpec(memory_space=pltpu.HBM),
            pl.BlockSpec(memory_space=pltpu.VMEM),
            pl.BlockSpec(memory_space=pltpu.VMEM),
            pl.BlockSpec(memory_space=pltpu.VMEM),
        ],
        out_specs=pl.BlockSpec(memory_space=pltpu.HBM),
        scratch_shapes=[
            pltpu.VMEM((3, (LAGS + 1) * rows, LANES), jnp.float32),
            pltpu.VMEM((UNITS + rows, LAG_ROWS, LANES), jnp.float32),
            pltpu.VMEM((3, LAGS, rows, LANES), jnp.bfloat16),
            pltpu.SemaphoreType.DMA((3,)),
        ],
        input_output_aliases={1: 0},
        compiler_params=pltpu.CompilerParams(vmem_limit_bytes=32 * MIB),
    )(info, begun, same, far, inverse)


def from_ahead(block, distance, parity=None):
    count = lax.axis_size("chan")
    route = [(i + distance, i) for i in range(count - distance) if parity is None or i % 2 == parity]
    return lax.ppermute(block, "chan", route)


def exchanged(block, axis):
    return lax.all_to_all(block, axis, split_axis=0, concat_axis=0, tiled=True)


def local(traces, window_starts, tile_offsets, tile_count):
    bands = lax.axis_size("band")
    rows = CB // bands
    width = HALF // bands
    forward, inverse = tables(bands)
    series = exchanged(traces, "chan")
    white = whitened_rows(window_starts, series, forward, bands)
    own = exchanged(white, "band")
    next1 = from_ahead(own, 1)
    next2 = (from_ahead(next1, 1, 0), from_ahead(own, 2, 1))
    reach = -(-(RANGE - 2 * CB) // rows)
    next3 = from_ahead(own[:reach], 3)
    near = near_cross(own, next1)
    near = exchanged(near, "band")
    far = vmem_call(
        far_kernel,
        (bands, rows + UNITS, 2 * width, LANES),
        [
            ((CB + 1) * 2 * width, LANES),
            ((bands + 1) * UNITS * 2 * width, LANES),
            ((CB + 1) * 2 * width, LANES),
        ],
        24 * MIB,
        own,
        *next2,
        next3,
    )
    white, far = lax.optimization_barrier((white, far))
    first = (lax.axis_index("band") * rows).astype(jnp.int32)[None]
    same = local_lags(first, white, from_ahead(white, 2), inverse)
    far = exchanged(far, "band")
    live = jnp.arange(TMAX) < tile_count[0]
    holds = (tile_offsets[0][None, :] == jnp.arange(TMAX)[:, None]) & live[None, :]
    slot_of = jnp.where(holds.any(axis=1), jnp.argmax(holds, axis=1), TMAX)
    reaches = first[0] + rows + RANGE > 3 * CB
    blank = ~live | (holds[3] & ~reaches)
    kind = jnp.where(blank, 2, jnp.where(holds[1], 1, 0))
    info = jnp.concatenate([slot_of, kind, first]).astype(jnp.int32)
    begun = first_lags(info, near, inverse)
    result = lags(info, begun, same, far, inverse)
    return result.transpose(0, 2, 3, 1)[None]


def solution(mesh):
    placed = (P(None, "band", "chan"), P(), P("chan", None), P("chan"))
    return jax.shard_map(
        local,
        mesh=mesh,
        in_specs=placed,
        out_specs=P("chan", None, "band", None, None),
        check_vma=False,
    )
```
